32 devices in a mesh: gx: 4 (over y, core), gy: 2 (over x), gz: 4 (over z).
Axes of the slice: x: 2, y: 2, z: 4, core: 2. Of those that a mesh axis runs over, the one named last changes fastest.
Arguments:
- source: float32 [32, 64, 512], P('gx', 'gy', 'gz'), may hold values from -24 to 24
- conductivity: float32 [32, 64, 512], P('gx', 'gy', 'gz'), may hold values from 0.2 to 5
Outputs:
- pressure: float32 [32, 64, 512], P('gx', 'gy', 'gz')
The draws below stay inside these ranges and needn't reach their ends.
All inputs are finite; a program needn't handle non-finite values.
Results may differ from the reference program's by a relative error of at most 0.00002.
Values sent between devices are 32-bit elements; how exact they have to be, the bound alone decides.
A program may use at most 64 MiB of HBM per device.

```python
import math
import jax
import jax.numpy as jnp
from jax import lax

CX = 8
CY = 32
CZ = 128
NX = 32
NY = 64
NZ = 512


def block_levels(key, extent, shards, low, top_value):
    gain, own = 1.0, jax.random.fold_in(key, 6)
    for dim, shards_of in shards:
        heights = jnp.exp(jax.random.uniform(jax.random.fold_in(own, dim), (shards_of,), jnp.float32, low / len(shards), top_value / len(shards)))
        gain = gain * jnp.repeat(heights, extent[dim] // shards_of).reshape([-1 if axis == dim else 1 for axis in range(len(extent))])
    return gain


def scatter_about(own_key, dims, width, limit, cuts=(), kind=jnp.bfloat16):
    array = jax.random.normal(own_key, dims, jnp.float32) * width
    if len(cuts) > 0:
        array = block_levels(own_key, dims, cuts, -0.22, 0.18) * array
    return jnp.clip(array, min=-limit, max=limit).astype(kind)


def setup_inputs(seed: int = 0) -> dict:
    key_list = jax.random.split(jax.random.key(seed), 3)
    source = scatter_about(key_list[0], (NX, NY, NZ), 4.0, 24.0, ((0, 4), (1, 2), (2, 4)), jnp.float32)
    conductivity = jnp.clip(jnp.exp(math.log(5.0) - 3.218876 * jax.random.uniform(key_list[1], (NX, NY, NZ), jnp.float32) ** block_levels(key_list[1], (NX, NY, NZ), ((0, 4), (1, 2), (2, 4)), -0.2, 0.2)), 0.2, 5.0)
    return {"source": source, "conductivity": conductivity}


spectrum_top = 1.9
spectrum_low = 0.475
omega_first = 1.0 / ((spectrum_top + spectrum_low) / 2 + (spectrum_top - spectrum_low) / 2 * math.cos(math.pi / 4))
omega_second = 1.0 / ((spectrum_top + spectrum_low) / 2 + (spectrum_top - spectrum_low) / 2 * math.cos(3 * math.pi / 4))
face_pairs = ((0, 1), (0, -1), (1, 1), (1, -1), (2, 1), (2, -1))


def interior(padded):
    return padded[1:-1, 1:-1, 1:-1]


def neighbour(padded, dimension, offset):
    starts = [1, 1, 1]
    limits = [padded.shape[0] - 1, padded.shape[1] - 1, padded.shape[2] - 1]
    starts[dimension] = 1 + offset
    limits[dimension] = padded.shape[dimension] - 1 + offset
    return lax.slice(padded, tuple(starts), tuple(limits))


def diagonal_of(coeff_pad):
    centre = interior(coeff_pad)
    result = jnp.zeros_like(centre)
    for dimension, offset in face_pairs:
        result = result + 0.5 * (centre + neighbour(coeff_pad, dimension, offset))
    return result


def operate(field_pad, coeff_pad):
    centre = interior(coeff_pad)
    values = interior(field_pad)
    result = jnp.zeros_like(centre)
    for dimension, offset in face_pairs:
        weight = 0.5 * (centre + neighbour(coeff_pad, dimension, offset))
        result = result + weight * (values - neighbour(field_pad, dimension, offset))
    return result


def sweep(field, field_pad, coeff_pad, rhs_field, diagonal, omega_value):
    return field + omega_value * (rhs_field - operate(field_pad, coeff_pad)) / diagonal


def restrict_axis(values, dimension):
    cells = (values.shape[dimension] - 2) // 2
    pieces = [lax.slice_in_dim(values, start_cell, start_cell + 2 * cells - 1, stride=2, axis=dimension) for start_cell in range(4)]
    return (pieces[0] + 3.0 * pieces[1] + 3.0 * pieces[2] + pieces[3]) * 0.125


def restrict(padded):
    return restrict_axis(restrict_axis(restrict_axis(padded, 0), 1), 2)


def interpolate_axis(values, dimension):
    cells = values.shape[dimension] - 2
    lower_side = lax.slice_in_dim(values, 0, cells, axis=dimension)
    centre = lax.slice_in_dim(values, 1, cells + 1, axis=dimension)
    upper_side = lax.slice_in_dim(values, 2, cells + 2, axis=dimension)
    even_cells = 0.75 * centre + 0.25 * lower_side
    odd_cells = 0.75 * centre + 0.25 * upper_side
    paired = jnp.stack([even_cells, odd_cells], axis=dimension + 1)
    new_shape = list(values.shape)
    new_shape[dimension] = 2 * cells
    return paired.reshape(tuple(new_shape))


def interpolate(padded):
    return interpolate_axis(interpolate_axis(interpolate_axis(padded, 0), 1), 2)


def coarsen(values):
    first, second, third = values.shape
    return values.reshape(first // 2, 2, second // 2, 2, third // 2, 2).mean(axis=(1, 3, 5))


def pad_zero(values):
    return jnp.pad(values, 1)


def box_correction(coeff_box, rhs_box):
    coeff_pad = pad_zero(coeff_box)
    diagonal = diagonal_of(coeff_pad)
    field = omega_first * rhs_box / diagonal
    field = sweep(field, pad_zero(field), coeff_pad, rhs_box, diagonal, omega_second)
    return interpolate(pad_zero(field))


def split_boxes(values, box_sizes):
    first, second, third = values.shape
    sized = values.reshape(first // box_sizes[0], box_sizes[0], second // box_sizes[1], box_sizes[1], third // box_sizes[2], box_sizes[2])
    return sized.transpose(0, 2, 4, 1, 3, 5).reshape(-1, box_sizes[0], box_sizes[1], box_sizes[2])


def join_boxes(boxes, box_counts):
    inner = boxes.shape[1:]
    sized = boxes.reshape(box_counts[0], box_counts[1], box_counts[2], inner[0], inner[1], inner[2])
    return sized.transpose(0, 3, 1, 4, 2, 5).reshape(box_counts[0] * inner[0], box_counts[1] * inner[1], box_counts[2] * inner[2])


def reference(source, conductivity):
    coeff_pad = pad_zero(conductivity)
    fine_diag = diagonal_of(coeff_pad)
    pressure = omega_first * source / fine_diag
    pressure = sweep(pressure, pad_zero(pressure), coeff_pad, source, fine_diag, omega_second)
    leftover = source - operate(pad_zero(pressure), coeff_pad)
    middle_rhs = 4.0 * restrict(pad_zero(leftover))
    middle_coeff = coarsen(conductivity)
    middle_pad = pad_zero(middle_coeff)
    middle_diag = diagonal_of(middle_pad)
    middle = omega_first * middle_rhs / middle_diag
    middle = sweep(middle, pad_zero(middle), middle_pad, middle_rhs, middle_diag, omega_second)
    middle_left = middle_rhs - operate(pad_zero(middle), middle_pad)
    coarse_rhs = 4.0 * restrict(pad_zero(middle_left))
    coarse_coeff = coarsen(middle_coeff)
    box_sizes = (CX // 2, CY // 2, CZ // 2)
    box_counts = tuple(coarse_coeff.shape[place] // box_sizes[place] for place in range(3))
    corrections = jax.vmap(box_correction)(split_boxes(coarse_coeff, box_sizes), split_boxes(coarse_rhs, box_sizes))
    middle = middle + join_boxes(corrections, box_counts)
    for omega_value in (omega_first, omega_second):
        middle = sweep(middle, pad_zero(middle), middle_pad, middle_rhs, middle_diag, omega_value)
    pressure = pressure + interpolate(pad_zero(middle))
    for omega_value in (omega_first, omega_second):
        pressure = sweep(pressure, pad_zero(pressure), coeff_pad, source, fine_diag, omega_value)
    return pressure
```

```python
import functools
import math

import jax
import jax.numpy as jnp
from jax import lax
from jax.experimental import pallas as pl
from jax.experimental.pallas import tpu as pltpu
from jax.sharding import PartitionSpec as P

spectrum_top = 1.9
spectrum_low = 0.475
omega_first = 1.0 / (
    (spectrum_top + spectrum_low) / 2 + (spectrum_top - spectrum_low) / 2 * math.cos(math.pi / 4)
)
omega_second = 1.0 / (
    (spectrum_top + spectrum_low) / 2
    + (spectrum_top - spectrum_low) / 2 * math.cos(3 * math.pi / 4)
)
F32 = jnp.float32
MESH = pl.DeviceIdType.MESH
H = 4
T = 8
copies = 40


def iota(shape, dim):
    return lax.broadcasted_iota(jnp.int32, shape, dim)


def dot(a, b):
    return jnp.dot(a, b, precision=lax.Precision.HIGHEST, preferred_element_type=F32)


def ring(index, size, cut):
    return jnp.where(index >= cut, index - size, index)


def restrict_weight(diff):
    side = (diff == -1) | (diff == 2)
    centre = (diff == 0) | (diff == 1)
    return jnp.where(centre, 0.375, jnp.where(side, 0.125, 0.0)).astype(F32)


def mean_weight(diff):
    return jnp.where((diff == 0) | (diff == 1), 0.5, 0.0).astype(F32)


def interpolate_weight(fine, coarse):
    base = (fine + 64) // 2 - 32
    other = base + jnp.where((fine + 64) % 2 == 0, -1, 1)
    return jnp.where(coarse == base, 0.75, jnp.where(coarse == other, 0.25, 0.0)).astype(F32)


def shift(values, axis, amount):
    size = values.shape[axis]
    return pltpu.roll(values, (-amount) % size, axis)


def kernel(
    sizes, s_ref, k_ref, out_ref,
    ks, pk, pa, pb, qe, wx, wy, wz, iv, ua, ub,
    own, ma, mb, mid, cz, cg, send_sem, recv_sem,
):
    cx, cy, cz_ = s_ref.shape
    hx, hy, hz = cx // 2, cy // 2, cz_ // 2
    qx, qy, qz = cx // 4, cy // 4, cz_ // 4
    ex, ey, ez = ks.shape[1:]
    mx, my, mz = mid.shape[1:]
    pos = {axis: lax.axis_index(axis) for axis in sizes}
    used = [0]

    def make(axis, way, src, dst, number):
        return pltpu.make_async_remote_copy(
            src_ref=src, dst_ref=dst, send_sem=send_sem.at[number], recv_sem=recv_sem.at[number],
            device_id={axis: pos[axis] + way}, device_id_type=MESH,
        )

    def has(axis, way):
        return pos[axis] < sizes[axis] - 1 if way > 0 else pos[axis] > 0

    def start(items):
        started = []
        for axis, way, src, dst in items:
            number = used[0]
            used[0] += 1
            started.append((axis, way, src, dst, number))

            @pl.when(has(axis, way))
            def _():
                make(axis, way, src, dst, number).start()

        return started

    def finish(started):
        for axis, way, src, dst, number in started:

            @pl.when(has(axis, way))
            def _():
                make(axis, way, src, dst, number).wait_send()

            @pl.when(has(axis, -way))
            def _():
                make(axis, way, src, dst, number).wait_recv()

    def pair(axis, src, dst):
        number = used[0]
        used[0] += 1
        mate = pos[axis] + 1 - 2 * (pos[axis] % 2)
        return pltpu.make_async_remote_copy(
            src_ref=src, dst_ref=dst, send_sem=send_sem.at[number], recv_sem=recv_sem.at[number],
            device_id={axis: mate}, device_id_type=MESH,
        )

    def clear(i, carry):
        ks[0, i] = jnp.zeros((ey, ez), F32)
        ks[1, i] = jnp.zeros((ey, ez), F32)
        return carry

    lax.fori_loop(0, ex, clear, 0)
    qe[...] = jnp.zeros(qe.shape, F32)
    pa[...] = jnp.zeros(pa.shape, F32)
    pb[...] = jnp.zeros(pb.shape, F32)
    mid[...] = jnp.zeros(mid.shape, F32)
    ma[...] = jnp.zeros(ma.shape, F32)
    mb[...] = jnp.zeros(mb.shape, F32)
    group = iota((cy, cz_), 1) // (2 * H)
    packed = jnp.zeros((cy, cz_), F32)
    for f, ref in enumerate((k_ref, s_ref)):
        for p in range(cx):
            g = f * cx + p
            packed = jnp.where(group == g, shift(ref[p], 1, -(H + 2 * H * g)), packed)
    pk[...] = packed

    barrier = pltpu.get_barrier_semaphore()
    count = 0
    for axis in sizes:
        for way in (1, -1):
            here = has(axis, way)
            count = count + here.astype(jnp.int32)

            @pl.when(here)
            def _():
                pl.semaphore_signal(
                    barrier, inc=1, device_id={axis: pos[axis] + way}, device_id_type=MESH
                )

    pl.semaphore_wait(barrier, count)

    main = pl.ds(0, cz_)
    rows = pl.ds(T, cy)
    items = [
        ("gz", 1, pk, pa),
        ("gz", -1, pk, pb),
    ]
    for f, ref in enumerate((k_ref, s_ref)):
        items += [
            ("gx", 1, ref.at[pl.ds(cx - H, H)], ks.at[f, pl.ds(0, H), rows, main]),
            ("gx", -1, ref.at[pl.ds(0, H)], ks.at[f, pl.ds(H + cx, H), rows, main]),
            ("gy", 1, ref.at[:, pl.ds(cy - T, T)], ks.at[f, pl.ds(H, cx), pl.ds(0, T), main]),
            ("gy", -1, ref.at[:, pl.ds(0, T)], ks.at[f, pl.ds(H, cx), pl.ds(T + cy, T), main]),
        ]
    first = start(items)
    for p in range(cx):
        ks[0, H + p, T : T + cy, 0:cz_] = k_ref[p]
        ks[1, H + p, T : T + cy, 0:cz_] = s_ref[p]
    finish(first[:2])
    lane = iota((cy, cz_), 1)
    qe[1, T : T + cy, :] = jnp.where(lane % (2 * H) < H, pa[...], pb[...])
    second = start([
        ("gx", 1, qe.at[1, rows], qe.at[0, rows]),
        ("gx", -1, qe.at[1, rows], qe.at[2, rows]),
    ])
    finish(first[2:])
    items = []
    for low in (0, H + cx):
        planes = pl.ds(low, H)
        items += [
            ("gy", 1, ks.at[:, planes, pl.ds(cy, T), main], ks.at[:, planes, pl.ds(0, T), main]),
            ("gy", -1, ks.at[:, planes, pl.ds(T, T), main], ks.at[:, planes, pl.ds(T + cy, T), main]),
        ]
    third = start(items)
    finish(second)
    fourth = start([
        ("gy", 1, qe.at[:, pl.ds(cy, T)], qe.at[:, pl.ds(0, T)]),
        ("gy", -1, qe.at[:, pl.ds(T, T)], qe.at[:, pl.ds(T + cy, T)]),
    ])
    finish(third)
    finish(fourth)
    for i in range(ex):
        block, p = (i - H) // cx + 1, (i - H) % cx
        for f in range(2):
            ks[f, i, :, cz_:ez] = shift(qe[block], 1, H + 2 * H * (f * cx + p))

    r = iota((ey, ez), 0) - T + pos["gy"] * cy
    local_z = ring(iota((ey, ez), 1), ez, ez - cz_ // 2)
    z = local_z + pos["gz"] * cz_
    fine_in = (r >= 0) & (r < cy * sizes["gy"]) & (z >= 0) & (z < cz_ * sizes["gz"])
    fine_in = fine_in & (local_z >= -H) & (local_z < cz_ + H)

    def plane_in(i):
        x = i - H + pos["gx"] * cx
        return (x >= 0) & (x < cx * sizes["gx"])

    wx[0] = 0.5 * (ks[0, 0] + ks[0, 1])

    def weights(i, carry):
        k = ks[0, i]
        after = 0.5 * (k + ks[0, i + 1])
        a = 0.5 * (k + shift(k, 0, 1))
        b = 0.5 * (k + shift(k, 1, 1))
        diag = (wx[i - 1] + after) + (a + shift(a, 0, -1)) + (b + shift(b, 1, -1))
        wx[i] = after
        wy[i] = a
        wz[i] = b
        inverse = jnp.where(fine_in & plane_in(i), 1.0 / diag, 0.0)
        iv[i] = inverse
        ua[i] = omega_first * ks[1, i] * inverse
        return carry

    lax.fori_loop(1, ex - 1, weights, 0)

    def around(u, i):
        v = u[i]
        a, b = wy[i], wz[i]
        total = wx[i] * u[i + 1] + wx[i - 1] * u[i - 1]
        total = total + (a * shift(v, 0, 1) + shift(a * v, 0, -1))
        total = total + (b * shift(v, 1, 1) + shift(b * v, 1, -1))
        return v, total

    def fine_sweep(u, i, omega):
        v, total = around(u, i)
        return (1.0 - omega) * v + omega * (ks[1, i] + total) * iv[i]

    def pre(i, carry):
        ub[i] = fine_sweep(ua, i, omega_second)
        return carry

    lax.fori_loop(2, ex - 2, pre, 0)

    def leftover(i, carry):
        v, total = around(ub, i)
        inverse = iv[i]
        diag = wx[i] + wx[i - 1] + (wy[i] + shift(wy[i], 0, -1)) + (wz[i] + shift(wz[i], 1, -1))
        ua[i] = jnp.where(inverse > 0.0, ks[1, i] - diag * v + total, 0.0)
        return carry

    lax.fori_loop(3, ex - 3, leftover, 0)

    lz = ring(iota((ez, mz), 0), ez, ez - cz_ // 2) - 2 * iota((ez, mz), 1)
    keep = iota((ez, mz), 1) < hz
    to_middle_z = jnp.where(keep, restrict_weight(lz), 0.0)
    mean_z = jnp.where(keep, mean_weight(lz), 0.0)
    ly = iota((hy, ey), 1) - T - 2 * iota((hy, ey), 0)
    to_middle_y, mean_y = restrict_weight(ly), mean_weight(ly)
    combined = []
    for i in range(hx):
        c = H + 2 * i
        combined.append((ua[c - 1] + ua[c + 2]) * 0.5 + (ua[c] + ua[c + 1]) * 1.5)
    stacked = dot(jnp.concatenate(combined, axis=0), to_middle_z)
    means = [(ks[0, H + 2 * i] + ks[0, H + 2 * i + 1]) * 0.5 for i in range(hx)]
    mean_stacked = dot(jnp.concatenate(means, axis=0), mean_z)
    for i in range(hx):
        own[0, i] = dot(mean_y, mean_stacked[i * ey : (i + 1) * ey])
        own[1, i] = dot(to_middle_y, stacked[i * ey : (i + 1) * ey])

    mrows = pl.ds(T, hy)
    mlane = iota((hy, mz), 1)

    def middle_exchange(fields, put):
        inside = pl.ds(fields[0], len(fields))
        step = start([
            ("gz", 1, own.at[inside], ma.at[inside]),
            ("gz", -1, own.at[inside], mb.at[inside]),
        ])
        finish(step)
        for f in fields:
            for i in range(hx):
                side = jnp.where(mlane < (mz - hz) // 2, mb[f, i], ma[f, i])
                put(f, i, jnp.where(mlane < hz, own[f, i], shift(side, 1, hz)))
        step = start([
            ("gx", 1, mid.at[inside, pl.ds(hx, hx), mrows], mid.at[inside, pl.ds(0, hx), mrows]),
            ("gx", -1, mid.at[inside, pl.ds(hx, hx), mrows], mid.at[inside, pl.ds(2 * hx, hx), mrows]),
        ])
        finish(step)
        step = start([
            ("gy", 1, mid.at[inside, :, pl.ds(hy, T)], mid.at[inside, :, pl.ds(0, T)]),
            ("gy", -1, mid.at[inside, :, pl.ds(T, T)], mid.at[inside, :, pl.ds(T + hy, T)]),
        ])
        finish(step)

    def put(f, i, values):
        mid[f, hx + i, T : T + hy, :] = values

    middle_exchange((0, 1), put)

    mr = iota((mx, my, mz), 1) - T + pos["gy"] * hy
    mlz = ring(iota((mx, my, mz), 2), mz, (hz + mz) // 2)
    mzz = mlz + pos["gz"] * hz
    mxx = iota((mx, my, mz), 0) - hx + pos["gx"] * hx
    middle_in = (
        (mr >= 0) & (mr < hy * sizes["gy"]) & (mzz >= 0) & (mzz < hz * sizes["gz"])
        & (mxx >= 0) & (mxx < hx * sizes["gx"]) & (mlz >= -H) & (mlz < hz + H)
    )

    def up(values):
        return jnp.concatenate([values[1:], values[:1]], axis=0)

    def down(values):
        return jnp.concatenate([values[-1:], values[:-1]], axis=0)

    def faces(k):
        return 0.5 * (k + up(k)), 0.5 * (k + shift(k, 1, 1)), 0.5 * (k + shift(k, 2, 1))

    def diagonal(w):
        return (w[0] + down(w[0])) + (w[1] + shift(w[1], 1, -1)) + (w[2] + shift(w[2], 2, -1))

    def neighbours(w, v):
        total = w[0] * up(v) + down(w[0] * v)
        total = total + (w[1] * shift(v, 1, 1) + shift(w[1] * v, 1, -1))
        return total + (w[2] * shift(v, 2, 1) + shift(w[2] * v, 2, -1))

    def sweep(w, inverse, v, f, omega):
        return (1.0 - omega) * v + omega * (f + neighbours(w, v)) * inverse

    mk, mf = mid[0], mid[1]
    mw = faces(mk)
    mdiag = diagonal(mw)
    miv = jnp.where(middle_in, 1.0 / mdiag, 0.0)
    m1 = omega_first * mf * miv
    m2 = sweep(mw, miv, m1, mf, omega_second)
    mleft = jnp.where(middle_in, mf - mdiag * m2 + neighbours(mw, m2), 0.0)

    px, py, pz = pos["gx"] % 2, pos["gy"] % 2, pos["gz"] % 2
    cj = iota((mz, mz), 1) - pz * qz
    clz = ring(iota((mz, mz), 0), mz, (hz + mz) // 2) - 2 * cj
    ckeep = (cj >= 0) & (cj < qz)
    to_coarse_z = jnp.where(ckeep, restrict_weight(clz), 0.0)
    cmean_z = jnp.where(ckeep, mean_weight(clz), 0.0)
    cly = iota((qy, my), 1) - T - 2 * iota((qy, my), 0)
    to_coarse_y, cmean_y = restrict_weight(cly), mean_weight(cly)
    for i in range(qx):
        c = hx + 2 * i
        mixed = (mleft[c - 1] + mleft[c + 2]) * 0.5 + (mleft[c] + mleft[c + 1]) * 1.5
        mean = (mk[c] + mk[c + 1]) * 0.5
        cz[0, 0, i] = dot(cmean_y, dot(mean, cmean_z))
        cz[0, 1, i] = dot(to_coarse_y, dot(mixed, to_coarse_z))
    copy = pair("gz", cz.at[0], cz.at[1])
    copy.start()
    copy.wait()
    here = pl.ds(px * qx, qx)
    line = pl.ds(pl.multiple_of(py * qy, qy), qy)
    cg[:, here, line, :] = cz[0] + cz[1]
    copy = pair("gy", cg.at[:, here, line], cg.at[:, here, line])
    copy.start()
    copy.wait()
    copy = pair("gx", cg.at[:, here], cg.at[:, here])
    copy.start()
    copy.wait()

    ck, cf = cg[0], cg[1]
    cshape = ck.shape
    row = iota(cshape, 1)
    plane = iota(cshape, 0)
    box_in = iota(cshape, 2) < 2 * qz
    cw = faces(ck)
    nx, ny = 2 * qx, 2 * qy
    half = 0.5 * ck
    cwx = jnp.where(plane < nx - 1, cw[0], 0.0)
    cwy = jnp.where(row < ny - 1, cw[1], 0.0)
    cw = (cwx, cwy, cw[2])
    cdiag = diagonal(cw)
    cdiag = cdiag + jnp.where(plane == 0, half, 0.0) + jnp.where(plane == nx - 1, half, 0.0)
    cdiag = cdiag + jnp.where(row == 0, half, 0.0) + jnp.where(row == ny - 1, half, 0.0)
    civ = jnp.where(box_in, 1.0 / cdiag, 0.0)
    c1 = omega_first * cf * civ
    c2 = sweep(cw, civ, c1, cf, omega_second)
    flat = c2.reshape(nx * ny, mz)
    jj = iota((mz, mz), 1)
    back_z = interpolate_weight(jj + pz * hz, iota((mz, mz), 0))
    back_z = jnp.where((jj < hz) & (iota((mz, mz), 0) < 2 * qz), back_z, 0.0)
    shape = (hx * hy, nx * ny)
    fine_i, coarse_i = iota(shape, 0), iota(shape, 1)
    back_xy = interpolate_weight(fine_i // hy + px * hx, coarse_i // ny) * interpolate_weight(
        fine_i % hy + py * hy, coarse_i % ny
    )
    correction = dot(back_xy, dot(flat, back_z))
    for i in range(hx):
        own[2, i] = m2[hx + i, T : T + hy, :] + correction[i * hy : (i + 1) * hy]
    middle_exchange((2,), put)
    m3 = mid[2]
    m4 = sweep(mw, miv, m3, mf, omega_first)
    m5 = sweep(mw, miv, m4, mf, omega_second)

    fine_lane = ring(iota((mz, ez), 1), ez, ez - cz_ // 2)
    middle_lane = ring(iota((mz, ez), 0), mz, (hz + mz) // 2)
    wide = (fine_lane >= -H) & (fine_lane < cz_ + H)
    to_fine_z = jnp.where(wide, interpolate_weight(fine_lane, middle_lane), 0.0)
    to_fine_y = interpolate_weight(iota((ey, my), 0) - T, iota((ey, my), 1) - T)
    mixed = []
    for i in range(2, ex - 2):
        c = (i - H + 64) // 2 - 32 + hx
        other = c - 1 if i % 2 == 0 else c + 1
        mixed.append(0.75 * m5[c] + 0.25 * m5[other])
    spread = dot(jnp.concatenate(mixed, axis=0), to_fine_z)
    for i in range(2, ex - 2):
        piece = spread[(i - 2) * my : (i - 1) * my]
        fresh = dot(to_fine_y, piece)
        ua[i] = jnp.where(fine_in & plane_in(i), ub[i] + fresh, 0.0)

    def post(i, carry):
        ub[i] = fine_sweep(ua, i, omega_first)
        return carry

    lax.fori_loop(3, ex - 3, post, 0)

    def last(i, carry):
        out_ref[i - H] = fine_sweep(ub, i, omega_second)[T : T + cy, 0:cz_]
        return carry

    lax.fori_loop(H, H + cx, last, 0)


def solution(mesh):
    sizes = {axis: mesh.shape[axis] for axis in mesh.axis_names}
    spec = P("gx", "gy", "gz")

    def local(source, conductivity):
        cx, cy, cz = source.shape
        fine = (cx + 2 * H, cy + 2 * T, 2 * cz)
        mid = (cx // 2 * 3, cy // 2 + 2 * T, cz)
        vmem = pltpu.VMEM
        call = pl.pallas_call(
            functools.partial(kernel, sizes),
            out_shape=jax.ShapeDtypeStruct(source.shape, F32),
            in_specs=[pl.BlockSpec(memory_space=vmem)] * 2,
            out_specs=pl.BlockSpec(memory_space=vmem),
            scratch_shapes=[
                vmem((2,) + fine, F32),
                vmem((cy, cz), F32),
                vmem((cy, cz), F32),
                vmem((cy, cz), F32),
                vmem((3, cy + 2 * T, cz), F32),
                vmem(fine, F32),
                vmem(fine, F32),
                vmem(fine, F32),
                vmem(fine, F32),
                vmem(fine, F32),
                vmem(fine, F32),
                vmem((3, cx // 2, cy // 2, cz), F32),
                vmem((3, cx // 2, cy // 2, cz), F32),
                vmem((3, cx // 2, cy // 2, cz), F32),
                vmem((3,) + mid, F32),
                vmem((2, 2, cx // 4, cy // 4, cz), F32),
                vmem((2, cx // 2, cy // 2, cz), F32),
                pltpu.SemaphoreType.DMA((copies,)),
                pltpu.SemaphoreType.DMA((copies,)),
            ],
            compiler_params=pltpu.CompilerParams(
                collective_id=0, has_side_effects=True, vmem_limit_bytes=48 * 2**20
            ),
        )
        return call(source, conductivity)

    return jax.shard_map(
        local, mesh=mesh, in_specs=(spec, spec), out_specs=spec, check_vma=False
    )
```

```python
import functools
import math

import jax
import jax.numpy as jnp
from jax import lax
from jax.experimental import pallas as pl
from jax.experimental.pallas import tpu as pltpu
from jax.sharding import PartitionSpec as P

spectrum_top = 1.9
spectrum_low = 0.475
omega_first = 1.0 / (
    (spectrum_top + spectrum_low) / 2 + (spectrum_top - spectrum_low) / 2 * math.cos(math.pi / 4)
)
omega_second = 1.0 / (
    (spectrum_top + spectrum_low) / 2
    + (spectrum_top - spectrum_low) / 2 * math.cos(3 * math.pi / 4)
)
F32 = jnp.float32
MESH = pl.DeviceIdType.MESH
H = 4
T = 8


def iota(shape, dim):
    return lax.broadcasted_iota(jnp.int32, shape, dim)


def parts(values):
    high = values.astype(jnp.bfloat16)
    rest = values - high.astype(F32)
    middle = rest.astype(jnp.bfloat16)
    return [high, middle, (rest - middle.astype(F32)).astype(jnp.bfloat16)]


def times(values, weights):
    size = values.shape[0]
    result = jnp.dot(
        jnp.concatenate(parts(values), axis=0),
        weights.astype(jnp.bfloat16),
        preferred_element_type=F32,
    )
    return result[:size] + (result[size : 2 * size] + result[2 * size :])


def weigh(weights, values):
    return jnp.dot(
        jnp.concatenate([weights.astype(jnp.bfloat16)] * 3, axis=1),
        jnp.concatenate(parts(values), axis=0),
        preferred_element_type=F32,
    )


def ring(index, size, cut):
    return jnp.where(index >= cut, index - size, index)


def restrict_weight(diff):
    side = (diff == -1) | (diff == 2)
    centre = (diff == 0) | (diff == 1)
    return jnp.where(centre, 0.375, jnp.where(side, 0.125, 0.0)).astype(F32)


def mean_weight(diff):
    return jnp.where((diff == 0) | (diff == 1), 0.5, 0.0).astype(F32)


def interpolate_weight(fine, coarse):
    base = (fine + 64) // 2 - 32
    other = base + jnp.where((fine + 64) % 2 == 0, -1, 1)
    return jnp.where(coarse == base, 0.75, jnp.where(coarse == other, 0.25, 0.0)).astype(F32)


def shift(values, axis, amount):
    size = values.shape[axis]
    return pltpu.roll(values, (-amount) % size, axis)


def span(way, extent, halo):
    if way == 0:
        return pl.ds(halo, extent), pl.ds(halo, extent)
    if way > 0:
        return pl.ds(extent, halo), pl.ds(0, halo)
    return pl.ds(halo, halo), pl.ds(halo + extent, halo)


ways = (0, 1, -1)
others = [(a, b, c) for c in ways for b in ways for a in ways if (a, b, c) != (0, 0, 0)]
mates = [(a, b, c) for a in (0, 1) for b in (0, 1) for c in (0, 1) if (a, b, c) != (0, 0, 0)]
axes = ("gx", "gy", "gz")
copies = 4 * len(others) + 2 * len(mates)


def kernel(
    sizes, s_ref, k_ref, out_ref,
    ks, pk, qa, qb, wx, wy, wz, iv, ua, ub, rs, fs, cs,
    mid, mp, ma, mb, cg, send_sem, recv_sem,
):
    cx, cy, cz_ = s_ref.shape
    hx, hy, hz = cx // 2, cy // 2, cz_ // 2
    qx, qy, qz = cx // 4, cy // 4, cz_ // 4
    ex, ey, ez = ks.shape[1:]
    mx, my, mz = mid.shape[1:]
    pos = {axis: lax.axis_index(axis) for axis in axes}
    used = [0]

    def has(offset, sign):
        here = None
        for axis, way in zip(axes, offset):
            if way != 0:
                good = pos[axis] < sizes[axis] - 1 if way * sign > 0 else pos[axis] > 0
                here = good if here is None else here & good
        return here

    def make(offset, src, dst, number):
        return pltpu.make_async_remote_copy(
            src_ref=src, dst_ref=dst, send_sem=send_sem.at[number], recv_sem=recv_sem.at[number],
            device_id={axis: pos[axis] + way for axis, way in zip(axes, offset)},
            device_id_type=MESH,
        )

    def start(items):
        started = []
        for offset, src, dst in items:
            number = used[0]
            used[0] += 1
            started.append((offset, src, dst, number))

            @pl.when(has(offset, 1))
            def _():
                make(offset, src, dst, number).start()

        return started

    def finish_recv(started):
        for offset, src, dst, number in started:

            @pl.when(has(offset, -1))
            def _():
                make(offset, src, dst, number).wait_recv()

    def finish_send(started):
        for offset, src, dst, number in started:

            @pl.when(has(offset, 1))
            def _():
                make(offset, src, dst, number).wait_send()

    def clear(i, carry):
        ks[0, i] = jnp.zeros((ey, ez), F32)
        ks[1, i] = jnp.zeros((ey, ez), F32)
        return carry

    lax.fori_loop(0, ex, clear, 0)
    qa[...] = jnp.zeros(qa.shape, F32)
    qb[...] = jnp.zeros(qb.shape, F32)
    mid[...] = jnp.zeros(mid.shape, F32)
    ma[...] = jnp.zeros(ma.shape, F32)
    mb[...] = jnp.zeros(mb.shape, F32)
    barrier = pltpu.get_barrier_semaphore()
    count = 0
    for offset in others:
        here = has(offset, 1)
        count = count + here.astype(jnp.int32)

        @pl.when(here)
        def _():
            pl.semaphore_signal(
                barrier, inc=1,
                device_id={axis: pos[axis] + way for axis, way in zip(axes, offset)},
                device_id_type=MESH,
            )

    group = iota((cy, cz_), 1) // (2 * H)
    packed = jnp.zeros((cy, cz_), F32)
    for f, ref in enumerate((k_ref, s_ref)):
        for p in range(cx):
            g = f * cx + p
            ks[f, H + p, T : T + cy, 0:cz_] = ref[p]
            packed = jnp.where(group == g, shift(ref[p], 1, -(H + 2 * H * g)), packed)
    pk[...] = packed
    pl.semaphore_wait(barrier, count)

    main = pl.ds(0, cz_)
    items = []
    for offset in others:
        dx, dy, dz = offset
        xs, xd = span(dx, cx, H)
        ys, yd = span(dy, cy, T)
        if dz == 0:
            items.append((offset, ks.at[:, xs, ys, main], ks.at[:, xd, yd, main]))
        else:
            target = qa if dz > 0 else qb
            rows = pl.ds(ys.start - T, ys.size)
            items.append((offset, pk.at[rows], target.at[1 - dx, yd]))
    fine_round = start(items)

    mgroup = iota((hy, mz), 1) // H

    def middle_start(f):
        packed = jnp.zeros((hy, mz), F32)
        for p in range(hx):
            own = mid[f, hx + p, T : T + hy, :]
            packed = jnp.where(mgroup == 2 * p, shift(own, 1, hz - H - 2 * H * p), packed)
            packed = jnp.where(mgroup == 2 * p + 1, shift(own, 1, -(2 * H * p + H)), packed)
        mp[f] = packed
        items = []
        for offset in others:
            dx, dy, dz = offset
            xs, xd = span(dx, hx, hx)
            ys, yd = span(dy, hy, T)
            if dz == 0:
                items.append((offset, mid.at[f, xs, ys], mid.at[f, xd, yd]))
            else:
                target = ma if dz > 0 else mb
                rows = pl.ds(ys.start - T, ys.size)
                items.append((offset, mp.at[f, rows], target.at[f, 1 - dx, yd]))
        return start(items)

    mlane = iota((my, mz), 1)

    def middle_finish(f, started):
        finish_recv(started)
        planes = []
        for i in range(mx):
            block, p = i // hx, i % hx
            right = shift(mb[f, block], 1, 2 * H * p + H - hz)
            left = shift(ma[f, block], 1, 2 * H * p - (mz - H))
            side = jnp.where(mlane < (hz + mz) // 2, right, left)
            planes.append(jnp.where(mlane < hz, mid[f, i], side)[None])
        return jnp.concatenate(planes, axis=0)

    px, py, pz = (pos[axis] % 2 for axis in axes)
    here = pl.ds(px * qx, qx)
    line = pl.ds(pl.multiple_of(py * qy, qy), qy)

    def gather_make(f, flips, number):
        return pltpu.make_async_remote_copy(
            src_ref=cg.at[f, 0, here, line], dst_ref=cg.at[f, flips[2], here, line],
            send_sem=send_sem.at[number], recv_sem=recv_sem.at[number],
            device_id={
                axis: pos[axis] + (1 - 2 * (pos[axis] % 2)) * flip for axis, flip in zip(axes, flips)
            },
            device_id_type=MESH,
        )

    def gather_start(f):
        started = []
        for flips in mates:
            copy = gather_make(f, flips, used[0])
            used[0] += 1
            copy.start()
            started.append(copy)
        return started

    lz = iota((cz_, mz), 0) - 2 * iota((cz_, mz), 1)
    mean_z = jnp.where(iota((cz_, mz), 1) < hz, mean_weight(lz), 0.0)
    for i in range(hx):
        rs[0, i, T : T + cy, :] = (k_ref[2 * i] + k_ref[2 * i + 1]) * 0.5
    means = [
        (rs[0, i, pl.ds(T, hy, stride=2), :] + rs[0, i, pl.ds(T + 1, hy, stride=2), :]) * 0.5
        for i in range(hx)
    ]
    means = times(jnp.concatenate(means, axis=0), mean_z)
    for i in range(hx):
        mid[0, hx + i, T : T + hy, :] = means[i * hy : (i + 1) * hy]
    coeff_round = middle_start(0)

    cj = iota((mz, mz), 1) - pz * qz
    clz = ring(iota((mz, mz), 0), mz, (hz + mz) // 2) - 2 * cj
    ckeep = (cj >= 0) & (cj < qz)
    to_coarse_z = jnp.where(ckeep, restrict_weight(clz), 0.0)
    cmean_z = jnp.where(ckeep, mean_weight(clz), 0.0)
    for i in range(qx):
        own_rows = [mid[0, hx + 2 * i + j, T : T + hy, :] for j in range(2)]
        cs[i, T : T + hy, :] = (own_rows[0] + own_rows[1]) * 0.5
    means = [
        (cs[i, pl.ds(T, qy, stride=2), :] + cs[i, pl.ds(T + 1, qy, stride=2), :]) * 0.5
        for i in range(qx)
    ]
    means = times(jnp.concatenate(means, axis=0), cmean_z)
    for i in range(qx):
        cg[0, 0, px * qx + i, line, :] = means[i * qy : (i + 1) * qy]
    gather_coeff = gather_start(0)

    r = iota((ey, ez), 0) - T + pos["gy"] * cy
    local_z = ring(iota((ey, ez), 1), ez, ez - cz_ // 2)
    z = local_z + pos["gz"] * cz_
    fine_in = (r >= 0) & (r < cy * sizes["gy"]) & (z >= 0) & (z < cz_ * sizes["gz"])
    fine_in = fine_in & (local_z >= -H) & (local_z < cz_ + H)

    def plane_in(i):
        x = i - H + pos["gx"] * cx
        return (x >= 0) & (x < cx * sizes["gx"])

    finish_recv(fine_round)
    lane = iota((ey, cz_), 1)
    for block in range(3):
        merged = jnp.where(lane % (2 * H) < H, qa[block], qb[block])
        for i in range(ex):
            if (i - H) // cx + 1 == block:
                for f in range(2):
                    p = (i - H) % cx
                    ks[f, i, :, cz_:ez] = shift(merged, 1, H + 2 * H * (f * cx + p))

    wx[0] = 0.5 * (ks[0, 0] + ks[0, 1])

    def weights(i, carry):
        k = ks[0, i]
        after = 0.5 * (k + ks[0, i + 1])
        a = 0.5 * (k + shift(k, 0, 1))
        b = 0.5 * (k + shift(k, 1, 1))
        diag = (wx[i - 1] + after) + (a + shift(a, 0, -1)) + (b + shift(b, 1, -1))
        wx[i] = after
        wy[i] = a
        wz[i] = b
        inverse = jnp.where(fine_in & plane_in(i), 1.0 / diag, 0.0)
        iv[i] = inverse
        ua[i] = omega_first * ks[1, i] * inverse
        return carry

    lax.fori_loop(1, ex - 1, weights, 0, unroll=2)

    def around(u, i):
        v = u[i]
        a, b = wy[i], wz[i]
        total = wx[i] * u[i + 1] + wx[i - 1] * u[i - 1]
        total = total + (a * shift(v, 0, 1) + shift(a * v, 0, -1))
        total = total + (b * shift(v, 1, 1) + shift(b * v, 1, -1))
        return v, total

    def fine_sweep(u, i, omega):
        v, total = around(u, i)
        return (1.0 - omega) * v + omega * (ks[1, i] + total) * iv[i]

    def pre(i, carry):
        ub[i] = fine_sweep(ua, i, omega_second)
        return carry

    lax.fori_loop(2, ex - 2, pre, 0, unroll=2)

    def leftover(i, carry):
        v, total = around(ub, i)
        inverse = iv[i]
        diag = wx[i] + wx[i - 1] + (wy[i] + shift(wy[i], 0, -1)) + (wz[i] + shift(wz[i], 1, -1))
        ua[i] = jnp.where(inverse > 0.0, ks[1, i] - diag * v + total, 0.0)
        return carry

    lax.fori_loop(3, ex - 3, leftover, 0, unroll=2)

    lz = ring(iota((ez, mz), 0), ez, ez - cz_ // 2) - 2 * iota((ez, mz), 1)
    to_middle_z = jnp.where(iota((ez, mz), 1) < hz, restrict_weight(lz), 0.0)

    def restrict_rows(take):
        side = take(T - 1) + take(T + 2)
        return side * 0.125 + (take(T) + take(T + 1)) * 0.375

    pieces = []
    for i in range(hx):
        c = H + 2 * i
        mixed = (ua[c - 1] + ua[c + 2]) * 0.5 + (ua[c] + ua[c + 1]) * 1.5
        rs[0, i] = mixed[:, :cz_]
        rs[1, i] = mixed[:, cz_:]
        halves = [
            restrict_rows(lambda first: rs[t, i, pl.ds(first, hy, stride=2), :]) for t in range(2)
        ]
        pieces.append(jnp.concatenate(halves, axis=1))
    rhs = times(jnp.concatenate(pieces, axis=0), to_middle_z)
    for i in range(hx):
        mid[1, hx + i, T : T + hy, :] = rhs[i * hy : (i + 1) * hy]
    rhs_round = middle_start(1)

    mr = iota((mx, my, mz), 1) - T + pos["gy"] * hy
    mlz = ring(iota((mx, my, mz), 2), mz, (hz + mz) // 2)
    mzz = mlz + pos["gz"] * hz
    mxx = iota((mx, my, mz), 0) - hx + pos["gx"] * hx
    middle_in = (
        (mr >= 0) & (mr < hy * sizes["gy"]) & (mzz >= 0) & (mzz < hz * sizes["gz"])
        & (mxx >= 0) & (mxx < hx * sizes["gx"]) & (mlz >= -H) & (mlz < hz + H)
    )

    def up(values):
        return jnp.concatenate([values[1:], values[:1]], axis=0)

    def down(values):
        return jnp.concatenate([values[-1:], values[:-1]], axis=0)

    def faces(k):
        return 0.5 * (k + up(k)), 0.5 * (k + shift(k, 1, 1)), 0.5 * (k + shift(k, 2, 1))

    def diagonal(w):
        return (w[0] + down(w[0])) + (w[1] + shift(w[1], 1, -1)) + (w[2] + shift(w[2], 2, -1))

    def neighbours(w, v):
        total = w[0] * up(v) + down(w[0] * v)
        total = total + (w[1] * shift(v, 1, 1) + shift(w[1] * v, 1, -1))
        return total + (w[2] * shift(v, 2, 1) + shift(w[2] * v, 2, -1))

    def sweep(w, inverse, v, f, omega):
        return (1.0 - omega) * v + omega * (f + neighbours(w, v)) * inverse

    mk = middle_finish(0, coeff_round)
    mw = faces(mk)
    mdiag = diagonal(mw)
    miv = jnp.where(middle_in, 1.0 / mdiag, 0.0)

    for copy in gather_coeff:
        copy.wait_recv()
    ck = cg[0, 0] + cg[0, 1]
    cshape = ck.shape
    row = iota(cshape, 1)
    plane = iota(cshape, 0)
    box_in = iota(cshape, 2) < 2 * qz
    nx, ny = 2 * qx, 2 * qy
    cw = faces(ck)
    half = 0.5 * ck
    cwx = jnp.where(plane < nx - 1, cw[0], 0.0)
    cwy = jnp.where(row < ny - 1, cw[1], 0.0)
    cw = (cwx, cwy, cw[2])
    cdiag = diagonal(cw)
    cdiag = cdiag + jnp.where(plane == 0, half, 0.0) + jnp.where(plane == nx - 1, half, 0.0)
    cdiag = cdiag + jnp.where(row == 0, half, 0.0) + jnp.where(row == ny - 1, half, 0.0)
    civ = jnp.where(box_in, 1.0 / cdiag, 0.0)

    mf = middle_finish(1, rhs_round)
    m1 = omega_first * mf * miv
    m2 = sweep(mw, miv, m1, mf, omega_second)
    mleft = jnp.where(middle_in, mf - mdiag * m2 + neighbours(mw, m2), 0.0)

    pieces = []
    for i in range(qx):
        c = hx + 2 * i
        cs[i] = (mleft[c - 1] + mleft[c + 2]) * 0.5 + (mleft[c] + mleft[c + 1]) * 1.5
        pieces.append(restrict_rows(lambda first: cs[i, pl.ds(first, qy, stride=2), :]))
    rhs = times(jnp.concatenate(pieces, axis=0), to_coarse_z)
    for i in range(qx):
        cg[1, 0, px * qx + i, line, :] = rhs[i * qy : (i + 1) * qy]
    gather_rhs = gather_start(1)
    for copy in gather_rhs:
        copy.wait_recv()

    cf = cg[1, 0] + cg[1, 1]
    c1 = omega_first * cf * civ
    c2 = sweep(cw, civ, c1, cf, omega_second)
    flat = c2.reshape(nx * ny, mz)
    jj = iota((mz, mz), 1)
    back_z = interpolate_weight(jj + pz * hz, iota((mz, mz), 0))
    back_z = jnp.where((jj < hz) & (iota((mz, mz), 0) < 2 * qz), back_z, 0.0)
    shape = (hx * hy, nx * ny)
    fine_i, coarse_i = iota(shape, 0), iota(shape, 1)
    back_xy = interpolate_weight(fine_i // hy + px * hx, coarse_i // ny) * interpolate_weight(
        fine_i % hy + py * hy, coarse_i % ny
    )
    correction = weigh(back_xy, times(flat, back_z))
    for i in range(hx):
        fixed = m2[hx + i, T : T + hy, :] + correction[i * hy : (i + 1) * hy]
        mid[2, hx + i, T : T + hy, :] = fixed
    last_round = middle_start(2)
    m3 = middle_finish(2, last_round)
    m4 = sweep(mw, miv, m3, mf, omega_first)
    m5 = sweep(mw, miv, m4, mf, omega_second)

    fine_lane = ring(iota((mz, ez), 1), ez, ez - cz_ // 2)
    middle_lane = ring(iota((mz, ez), 0), mz, (hz + mz) // 2)
    wide = (fine_lane >= -H) & (fine_lane < cz_ + H)
    to_fine_z = jnp.where(wide, interpolate_weight(fine_lane, middle_lane), 0.0)
    low = hx - 2
    spread = times(m5[low : 2 * hx + 2].reshape((hx + 4) * my, mz), to_fine_z)
    for i in range(2, ex - 2):
        c = (i - H + 64) // 2 - 32 + hx - low
        other = c - 1 if i % 2 == 0 else c + 1
        mixed = 0.75 * spread[c * my : (c + 1) * my] + 0.25 * spread[other * my : (other + 1) * my]
        near = 0.75 * mixed
        even = near + 0.25 * shift(mixed, 0, -1)
        odd = near + 0.25 * shift(mixed, 0, 1)
        for t in range(2):
            lanes = slice(t * cz_, (t + 1) * cz_)
            fs[t, i - 2, pl.ds(0, my, stride=2), :] = even[:, lanes]
            fs[t, i - 2, pl.ds(1, my, stride=2), :] = odd[:, lanes]
    for i in range(2, ex - 2):
        rows = slice(2 * T - T, 2 * T - T + ey)
        fresh = jnp.concatenate([fs[0, i - 2, rows, :], fs[1, i - 2, rows, :]], axis=1)
        ua[i] = jnp.where(fine_in & plane_in(i), ub[i] + fresh, 0.0)

    def post(i, carry):
        ub[i] = fine_sweep(ua, i, omega_first)
        return carry

    lax.fori_loop(3, ex - 3, post, 0, unroll=2)

    def last(i, carry):
        out_ref[i - H] = fine_sweep(ub, i, omega_second)[T : T + cy, 0:cz_]
        return carry

    lax.fori_loop(H, H + cx, last, 0, unroll=2)
    for started in (fine_round, coeff_round, rhs_round, last_round):
        finish_send(started)
    for copy in gather_coeff + gather_rhs:
        copy.wait_send()


def solution(mesh):
    sizes = {axis: mesh.shape[axis] for axis in mesh.axis_names}
    spec = P("gx", "gy", "gz")

    def local(source, conductivity):
        cx, cy, cz = source.shape
        fine = (cx + 2 * H, cy + 2 * T, 2 * cz)
        mid = (cx // 2 * 3, cy // 2 + 2 * T, cz)
        vmem = pltpu.VMEM
        call = pl.pallas_call(
            functools.partial(kernel, sizes),
            out_shape=jax.ShapeDtypeStruct(source.shape, F32),
            in_specs=[pl.BlockSpec(memory_space=vmem)] * 2,
            out_specs=pl.BlockSpec(memory_space=vmem),
            scratch_shapes=[
                vmem((2,) + fine, F32),
                vmem((cy, cz), F32),
                vmem((3, cy + 2 * T, cz), F32),
                vmem((3, cy + 2 * T, cz), F32),
                vmem(fine, F32),
                vmem(fine, F32),
                vmem(fine, F32),
                vmem(fine, F32),
                vmem(fine, F32),
                vmem(fine, F32),
                vmem((2, cx // 2, cy + 2 * T, cz), F32),
                vmem((2, cx + 4, 2 * mid[1], cz), F32),
                vmem((cx // 4, mid[1], cz), F32),
                vmem((3,) + mid, F32),
                vmem((3, cy // 2, cz), F32),
                vmem((3, 3) + mid[1:], F32),
                vmem((3, 3) + mid[1:], F32),
                vmem((2, 2, cx // 2, cy // 2, cz), F32),
                pltpu.SemaphoreType.DMA((copies,)),
                pltpu.SemaphoreType.DMA((copies,)),
            ],
            compiler_params=pltpu.CompilerParams(
                collective_id=0, has_side_effects=True, vmem_limit_bytes=48 * 2**20
            ),
        )
        return call(source, conductivity)

    return jax.shard_map(
        local, mesh=mesh, in_specs=(spec, spec), out_specs=spec, check_vma=False
    )
```

```python
import functools
import math

import jax
import jax.numpy as jnp
from jax import lax
from jax.experimental import pallas as pl
from jax.experimental.pallas import tpu as pltpu
from jax.sharding import PartitionSpec as P

spectrum_top = 1.9
spectrum_low = 0.475
omega_first = 1.0 / (
    (spectrum_top + spectrum_low) / 2 + (spectrum_top - spectrum_low) / 2 * math.cos(math.pi / 4)
)
omega_second = 1.0 / (
    (spectrum_top + spectrum_low) / 2
    + (spectrum_top - spectrum_low) / 2 * math.cos(3 * math.pi / 4)
)
F32 = jnp.float32
MESH = pl.DeviceIdType.MESH
H = 4
T = 8


def iota(shape, dim):
    return lax.broadcasted_iota(jnp.int32, shape, dim)


def parts(values):
    high = values.astype(jnp.bfloat16)
    rest = values - high.astype(F32)
    middle = rest.astype(jnp.bfloat16)
    return [high, middle, (rest - middle.astype(F32)).astype(jnp.bfloat16)]


def times(values, weights):
    size = values.shape[0]
    result = jnp.dot(
        jnp.concatenate(parts(values), axis=0),
        weights.astype(jnp.bfloat16),
        preferred_element_type=F32,
    )
    return result[:size] + (result[size : 2 * size] + result[2 * size :])


def weigh(weights, values):
    return jnp.dot(
        jnp.concatenate([weights.astype(jnp.bfloat16)] * 3, axis=1),
        jnp.concatenate(parts(values), axis=0),
        preferred_element_type=F32,
    )


def ring(index, size, cut):
    return jnp.where(index >= cut, index - size, index)


def restrict_weight(diff):
    side = (diff == -1) | (diff == 2)
    centre = (diff == 0) | (diff == 1)
    return jnp.where(centre, 0.375, jnp.where(side, 0.125, 0.0)).astype(F32)


def mean_weight(diff):
    return jnp.where((diff == 0) | (diff == 1), 0.5, 0.0).astype(F32)


def interpolate_weight(fine, coarse):
    base = (fine + 64) // 2 - 32
    other = base + jnp.where((fine + 64) % 2 == 0, -1, 1)
    return jnp.where(coarse == base, 0.75, jnp.where(coarse == other, 0.25, 0.0)).astype(F32)


def shift(values, axis, amount):
    size = values.shape[axis]
    return pltpu.roll(values, (-amount) % size, axis)


def span(way, extent, halo):
    if way == 0:
        return pl.ds(halo, extent), pl.ds(halo, extent)
    if way > 0:
        return pl.ds(extent, halo), pl.ds(0, halo)
    return pl.ds(halo, halo), pl.ds(halo + extent, halo)


ways = (0, 1, -1)
others = [(a, b, c) for c in ways for b in ways for a in ways if (a, b, c) != (0, 0, 0)]
mates = [(a, b, c) for a in (0, 1) for b in (0, 1) for c in (0, 1) if (a, b, c) != (0, 0, 0)]
axes = ("gx", "gy", "gz")
copies = 4 * len(others) + 2 * len(mates)


def kernel(
    sizes, s_ref, k_ref, out_ref,
    ks, pk, qa, qb, wx, wy, wz, iv, ua, ub, left, rs, fs, cs,
    mid, mp, ma, mb, cg, send_sem, recv_sem, load_sem,
):
    cx, cy, cz_ = s_ref.shape
    hx, hy, hz = cx // 2, cy // 2, cz_ // 2
    qx, qy, qz = cx // 4, cy // 4, cz_ // 4
    ex, ey, ez = ks.shape[1:]
    mx, my, mz = mid.shape[1:]
    pos = {axis: lax.axis_index(axis) for axis in axes}
    used = [0]

    def has(offset, sign):
        here = None
        for axis, way in zip(axes, offset):
            if way != 0:
                good = pos[axis] < sizes[axis] - 1 if way * sign > 0 else pos[axis] > 0
                here = good if here is None else here & good
        return here

    def make(offset, src, dst, number):
        return pltpu.make_async_remote_copy(
            src_ref=src, dst_ref=dst, send_sem=send_sem.at[number], recv_sem=recv_sem.at[number],
            device_id={axis: pos[axis] + way for axis, way in zip(axes, offset)},
            device_id_type=MESH,
        )

    def start(items):
        started = []
        for offset, src, dst in items:
            number = used[0]
            used[0] += 1
            started.append((offset, src, dst, number))

            @pl.when(has(offset, 1))
            def _():
                make(offset, src, dst, number).start()

        return started

    def finish_recv(started, wanted=lambda offset: True):
        for offset, src, dst, number in started:
            if not wanted(offset):
                continue

            @pl.when(has(offset, -1))
            def _():
                make(offset, src, dst, number).wait_recv()

    def finish_send(started):
        for offset, src, dst, number in started:

            @pl.when(has(offset, 1))
            def _():
                make(offset, src, dst, number).wait_send()

    loads = []
    for f, ref in enumerate((k_ref, s_ref)):
        own = ks.at[f, pl.ds(H, cx), pl.ds(T, cy), pl.ds(0, cz_)]
        loads.append(pltpu.make_async_copy(ref, own, load_sem.at[f]))
        loads[f].start()
    for f in range(2):
        for i in range(ex):
            if H <= i < H + cx:
                ks[f, i, 0:T, 0:cz_] = jnp.zeros((T, cz_), F32)
                ks[f, i, T + cy : ey, 0:cz_] = jnp.zeros((T, cz_), F32)
            else:
                ks[f, i, :, 0:cz_] = jnp.zeros((ey, cz_), F32)
    qa[...] = jnp.zeros(qa.shape, F32)
    qb[...] = jnp.zeros(qb.shape, F32)
    mid[...] = jnp.zeros(mid.shape, F32)
    ma[...] = jnp.zeros(ma.shape, F32)
    mb[...] = jnp.zeros(mb.shape, F32)
    barrier = pltpu.get_barrier_semaphore()
    count = 0
    for offset in others:
        here = has(offset, 1)
        count = count + here.astype(jnp.int32)

        @pl.when(here)
        def _():
            pl.semaphore_signal(
                barrier, inc=1,
                device_id={axis: pos[axis] + way for axis, way in zip(axes, offset)},
                device_id_type=MESH,
            )

    group = iota((cy, cz_), 1) // (2 * H)
    packed = jnp.zeros((cy, cz_), F32)
    for f in range(2):
        loads[f].wait()
        for p in range(cx):
            g = f * cx + p
            own = ks[f, H + p, T : T + cy, 0:cz_]
            packed = jnp.where(group == g, shift(own, 1, -(H + 2 * H * g)), packed)
    pk[...] = packed
    pl.semaphore_wait(barrier, count)

    main = pl.ds(0, cz_)
    items = []
    for offset in others:
        dx, dy, dz = offset
        xs, xd = span(dx, cx, H)
        ys, yd = span(dy, cy, T)
        if dz == 0:
            items.append((offset, ks.at[:, xs, ys, main], ks.at[:, xd, yd, main]))
        else:
            target = qa if dz > 0 else qb
            rows = pl.ds(ys.start - T, ys.size)
            items.append((offset, pk.at[rows], target.at[1 - dx, yd]))
    fine_round = start(items)

    mgroup = iota((hy, mz), 1) // H

    def middle_start(f):
        packed = jnp.zeros((hy, mz), F32)
        for p in range(hx):
            own = mid[f, hx + p, T : T + hy, :]
            packed = jnp.where(mgroup == 2 * p, shift(own, 1, hz - H - 2 * H * p), packed)
            packed = jnp.where(mgroup == 2 * p + 1, shift(own, 1, -(2 * H * p + H)), packed)
        mp[f] = packed
        items = []
        for offset in others:
            dx, dy, dz = offset
            xs, xd = span(dx, hx, hx)
            ys, yd = span(dy, hy, T)
            if dz == 0:
                items.append((offset, mid.at[f, xs, ys], mid.at[f, xd, yd]))
            else:
                target = ma if dz > 0 else mb
                rows = pl.ds(ys.start - T, ys.size)
                items.append((offset, mp.at[f, rows], target.at[f, 1 - dx, yd]))
        return start(items)

    mlane = iota((my, mz), 1)

    def middle_finish(f, started):
        finish_recv(started)
        planes = []
        for i in range(mx):
            block, p = i // hx, i % hx
            right = shift(mb[f, block], 1, 2 * H * p + H - hz)
            left = shift(ma[f, block], 1, 2 * H * p - (mz - H))
            side = jnp.where(mlane < (hz + mz) // 2, right, left)
            planes.append(jnp.where(mlane < hz, mid[f, i], side)[None])
        return jnp.concatenate(planes, axis=0)

    px, py, pz = (pos[axis] % 2 for axis in axes)
    here = pl.ds(px * qx, qx)
    line = pl.ds(pl.multiple_of(py * qy, qy), qy)

    def gather_make(f, flips, number):
        return pltpu.make_async_remote_copy(
            src_ref=cg.at[f, 0, here, line], dst_ref=cg.at[f, flips[2], here, line],
            send_sem=send_sem.at[number], recv_sem=recv_sem.at[number],
            device_id={
                axis: pos[axis] + (1 - 2 * (pos[axis] % 2)) * flip for axis, flip in zip(axes, flips)
            },
            device_id_type=MESH,
        )

    def gather_start(f):
        started = []
        for flips in mates:
            copy = gather_make(f, flips, used[0])
            used[0] += 1
            copy.start()
            started.append(copy)
        return started

    lz = iota((cz_, mz), 0) - 2 * iota((cz_, mz), 1)
    mean_z = jnp.where(iota((cz_, mz), 1) < hz, mean_weight(lz), 0.0)
    for i in range(hx):
        own = [ks[0, H + 2 * i + j, T : T + cy, 0:cz_] for j in range(2)]
        rs[0, i, T : T + cy, :] = (own[0] + own[1]) * 0.5
    means = [
        (rs[0, i, pl.ds(T, hy, stride=2), :] + rs[0, i, pl.ds(T + 1, hy, stride=2), :]) * 0.5
        for i in range(hx)
    ]
    means = times(jnp.concatenate(means, axis=0), mean_z)
    for i in range(hx):
        mid[0, hx + i, T : T + hy, :] = means[i * hy : (i + 1) * hy]
    coeff_round = middle_start(0)

    cj = iota((mz, mz), 1) - pz * qz
    clz = ring(iota((mz, mz), 0), mz, (hz + mz) // 2) - 2 * cj
    ckeep = (cj >= 0) & (cj < qz)
    to_coarse_z = jnp.where(ckeep, restrict_weight(clz), 0.0)
    cmean_z = jnp.where(ckeep, mean_weight(clz), 0.0)
    for i in range(qx):
        own_rows = [mid[0, hx + 2 * i + j, T : T + hy, :] for j in range(2)]
        cs[i, T : T + hy, :] = (own_rows[0] + own_rows[1]) * 0.5
    means = [
        (cs[i, pl.ds(T, qy, stride=2), :] + cs[i, pl.ds(T + 1, qy, stride=2), :]) * 0.5
        for i in range(qx)
    ]
    means = times(jnp.concatenate(means, axis=0), cmean_z)
    for i in range(qx):
        cg[0, 0, px * qx + i, line, :] = means[i * qy : (i + 1) * qy]
    gather_coeff = gather_start(0)

    r = iota((ey, ez), 0) - T + pos["gy"] * cy
    local_z = ring(iota((ey, ez), 1), ez, ez - cz_ // 2)
    z = local_z + pos["gz"] * cz_
    fine_in = (r >= 0) & (r < cy * sizes["gy"]) & (z >= 0) & (z < cz_ * sizes["gz"])
    fine_in = fine_in & (local_z >= -H) & (local_z < cz_ + H)

    def plane_in(i):
        x = i - H + pos["gx"] * cx
        return (x >= 0) & (x < cx * sizes["gx"])

    lz = ring(iota((ez, mz), 0), ez, ez - cz_ // 2) - 2 * iota((ez, mz), 1)
    to_middle_z = jnp.where(iota((ez, mz), 1) < hz, restrict_weight(lz), 0.0)

    mr = iota((mx, my, mz), 1) - T + pos["gy"] * hy
    mlz = ring(iota((mx, my, mz), 2), mz, (hz + mz) // 2)
    mzz = mlz + pos["gz"] * hz
    mxx = iota((mx, my, mz), 0) - hx + pos["gx"] * hx
    middle_in = (
        (mr >= 0) & (mr < hy * sizes["gy"]) & (mzz >= 0) & (mzz < hz * sizes["gz"])
        & (mxx >= 0) & (mxx < hx * sizes["gx"]) & (mlz >= -H) & (mlz < hz + H)
    )

    jj = iota((mz, mz), 1)
    back_z = interpolate_weight(jj + pz * hz, iota((mz, mz), 0))
    back_z = jnp.where((jj < hz) & (iota((mz, mz), 0) < 2 * qz), back_z, 0.0)
    shape = (hx * hy, 4 * qx * qy)
    fine_i, coarse_i = iota(shape, 0), iota(shape, 1)
    back_xy = interpolate_weight(fine_i // hy + px * hx, coarse_i // (2 * qy)) * interpolate_weight(
        fine_i % hy + py * hy, coarse_i % (2 * qy)
    )
    fine_lane = ring(iota((mz, ez), 1), ez, ez - cz_ // 2)
    middle_lane = ring(iota((mz, ez), 0), mz, (hz + mz) // 2)
    wide = (fine_lane >= -H) & (fine_lane < cz_ + H)
    to_fine_z = jnp.where(wide, interpolate_weight(fine_lane, middle_lane), 0.0)

    lane = iota((ey, cz_), 1)

    def unpack(block):
        merged = jnp.where(lane % (2 * H) < H, qa[block], qb[block])
        for i in range(ex):
            if (i - H) // cx + 1 == block:
                for f in range(2):
                    p = (i - H) % cx
                    ks[f, i, :, cz_:ez] = shift(merged, 1, H + 2 * H * (f * cx + p))

    def weights(i, carry):
        k = ks[0, i]
        after = 0.5 * (k + ks[0, i + 1])
        a = 0.5 * (k + shift(k, 0, 1))
        b = 0.5 * (k + shift(k, 1, 1))
        diag = (wx[i - 1] + after) + (a + shift(a, 0, -1)) + (b + shift(b, 1, -1))
        wx[i] = after
        wy[i] = a
        wz[i] = b
        inverse = jnp.where(fine_in & plane_in(i), 1.0 / diag, 0.0)
        iv[i] = inverse
        ua[i] = omega_first * ks[1, i] * inverse
        return carry

    def around(u, i):
        v = u[i]
        a, b = wy[i], wz[i]
        total = wx[i] * u[i + 1] + wx[i - 1] * u[i - 1]
        total = total + (a * shift(v, 0, 1) + shift(a * v, 0, -1))
        total = total + (b * shift(v, 1, 1) + shift(b * v, 1, -1))
        return v, total

    def fine_sweep(u, i, omega):
        v, total = around(u, i)
        return (1.0 - omega) * v + omega * (ks[1, i] + total) * iv[i]

    def pre(i, carry):
        ub[i] = fine_sweep(ua, i, omega_second)
        return carry


    def leftover(i, carry):
        v, total = around(ub, i)
        inverse = iv[i]
        diag = wx[i] + wx[i - 1] + (wy[i] + shift(wy[i], 0, -1)) + (wz[i] + shift(wz[i], 1, -1))
        left[i] = jnp.where(inverse > 0.0, ks[1, i] - diag * v + total, 0.0)
        return carry

    def run(low, high, body):
        lax.fori_loop(low, high, body, 0, unroll=2)

    last_own = H + cx - 1
    finish_recv(fine_round, lambda offset: offset[0] == 0)
    unpack(1)
    wx[H] = 0.5 * (ks[0, H] + ks[0, H + 1])
    run(H + 1, last_own, weights)
    run(H + 2, last_own - 1, pre)
    run(H + 3, last_own - 2, leftover)
    finish_recv(fine_round, lambda offset: offset[0] != 0)
    unpack(0)
    unpack(2)
    wx[0] = 0.5 * (ks[0, 0] + ks[0, 1])
    run(1, H + 1, weights)
    run(last_own, ex - 1, weights)
    run(2, H + 2, pre)
    run(last_own - 1, ex - 2, pre)
    run(3, H + 3, leftover)
    run(last_own - 2, ex - 3, leftover)

    def restrict_rows(take):
        side = take(T - 1) + take(T + 2)
        return side * 0.125 + (take(T) + take(T + 1)) * 0.375

    pieces = []
    for i in range(hx):
        c = H + 2 * i
        mixed = (left[c - 1] + left[c + 2]) * 0.5 + (left[c] + left[c + 1]) * 1.5
        rs[0, i] = mixed[:, :cz_]
        rs[1, i] = mixed[:, cz_:]
        halves = [
            restrict_rows(lambda first: rs[t, i, pl.ds(first, hy, stride=2), :]) for t in range(2)
        ]
        pieces.append(jnp.concatenate(halves, axis=1))
    rhs = times(jnp.concatenate(pieces, axis=0), to_middle_z)
    for i in range(hx):
        mid[1, hx + i, T : T + hy, :] = rhs[i * hy : (i + 1) * hy]
    rhs_round = middle_start(1)

    def up(values):
        return jnp.concatenate([values[1:], values[:1]], axis=0)

    def down(values):
        return jnp.concatenate([values[-1:], values[:-1]], axis=0)

    def faces(k):
        return 0.5 * (k + up(k)), 0.5 * (k + shift(k, 1, 1)), 0.5 * (k + shift(k, 2, 1))

    def diagonal(w):
        return (w[0] + down(w[0])) + (w[1] + shift(w[1], 1, -1)) + (w[2] + shift(w[2], 2, -1))

    def neighbours(w, v):
        total = w[0] * up(v) + down(w[0] * v)
        total = total + (w[1] * shift(v, 1, 1) + shift(w[1] * v, 1, -1))
        return total + (w[2] * shift(v, 2, 1) + shift(w[2] * v, 2, -1))

    def sweep(w, inverse, v, f, omega):
        return (1.0 - omega) * v + omega * (f + neighbours(w, v)) * inverse

    mk = middle_finish(0, coeff_round)
    mw = faces(mk)
    mdiag = diagonal(mw)
    miv = jnp.where(middle_in, 1.0 / mdiag, 0.0)

    for copy in gather_coeff:
        copy.wait_recv()
    ck = cg[0, 0] + cg[0, 1]
    cshape = ck.shape
    row = iota(cshape, 1)
    plane = iota(cshape, 0)
    box_in = iota(cshape, 2) < 2 * qz
    nx, ny = 2 * qx, 2 * qy
    cw = faces(ck)
    half = 0.5 * ck
    cwx = jnp.where(plane < nx - 1, cw[0], 0.0)
    cwy = jnp.where(row < ny - 1, cw[1], 0.0)
    cw = (cwx, cwy, cw[2])
    cdiag = diagonal(cw)
    cdiag = cdiag + jnp.where(plane == 0, half, 0.0) + jnp.where(plane == nx - 1, half, 0.0)
    cdiag = cdiag + jnp.where(row == 0, half, 0.0) + jnp.where(row == ny - 1, half, 0.0)
    civ = jnp.where(box_in, 1.0 / cdiag, 0.0)

    finish_send(fine_round)
    finish_send(coeff_round)
    for copy in gather_coeff:
        copy.wait_send()
    mf = middle_finish(1, rhs_round)
    m1 = omega_first * mf * miv
    m2 = sweep(mw, miv, m1, mf, omega_second)
    mleft = jnp.where(middle_in, mf - mdiag * m2 + neighbours(mw, m2), 0.0)

    pieces = []
    for i in range(qx):
        c = hx + 2 * i
        cs[i] = (mleft[c - 1] + mleft[c + 2]) * 0.5 + (mleft[c] + mleft[c + 1]) * 1.5
        pieces.append(restrict_rows(lambda first: cs[i, pl.ds(first, qy, stride=2), :]))
    rhs = times(jnp.concatenate(pieces, axis=0), to_coarse_z)
    for i in range(qx):
        cg[1, 0, px * qx + i, line, :] = rhs[i * qy : (i + 1) * qy]
    gather_rhs = gather_start(1)
    finish_send(rhs_round)
    for copy in gather_rhs:
        copy.wait_recv()

    cf = cg[1, 0] + cg[1, 1]
    c1 = omega_first * cf * civ
    c2 = sweep(cw, civ, c1, cf, omega_second)
    flat = c2.reshape(nx * ny, mz)
    correction = weigh(back_xy, times(flat, back_z))
    for i in range(hx):
        fixed = m2[hx + i, T : T + hy, :] + correction[i * hy : (i + 1) * hy]
        mid[2, hx + i, T : T + hy, :] = fixed
    last_round = middle_start(2)
    for copy in gather_rhs:
        copy.wait_send()
    m3 = middle_finish(2, last_round)
    m4 = sweep(mw, miv, m3, mf, omega_first)
    m5 = sweep(mw, miv, m4, mf, omega_second)

    low = hx - 2
    spread = times(m5[low : 2 * hx + 2].reshape((hx + 4) * my, mz), to_fine_z)
    for i in range(2, ex - 2):
        c = (i - H + 64) // 2 - 32 + hx - low
        other = c - 1 if i % 2 == 0 else c + 1
        mixed = 0.75 * spread[c * my : (c + 1) * my] + 0.25 * spread[other * my : (other + 1) * my]
        near = 0.75 * mixed
        even = near + 0.25 * shift(mixed, 0, -1)
        odd = near + 0.25 * shift(mixed, 0, 1)
        for t in range(2):
            lanes = slice(t * cz_, (t + 1) * cz_)
            fs[t, i - 2, pl.ds(0, my, stride=2), :] = even[:, lanes]
            fs[t, i - 2, pl.ds(1, my, stride=2), :] = odd[:, lanes]
    for i in range(2, ex - 2):
        rows = slice(2 * T - T, 2 * T - T + ey)
        fresh = jnp.concatenate([fs[0, i - 2, rows, :], fs[1, i - 2, rows, :]], axis=1)
        ua[i] = jnp.where(fine_in & plane_in(i), ub[i] + fresh, 0.0)

    def post(i, carry):
        ub[i] = fine_sweep(ua, i, omega_first)
        return carry

    lax.fori_loop(3, ex - 3, post, 0, unroll=2)

    def last(i, carry):
        out_ref[i - H] = fine_sweep(ub, i, omega_second)[T : T + cy, 0:cz_]
        return carry

    lax.fori_loop(H, H + cx, last, 0, unroll=2)
    finish_send(last_round)


def solution(mesh):
    sizes = {axis: mesh.shape[axis] for axis in mesh.axis_names}
    spec = P("gx", "gy", "gz")

    def local(source, conductivity):
        cx, cy, cz = source.shape
        fine = (cx + 2 * H, cy + 2 * T, 2 * cz)
        mid = (cx // 2 * 3, cy // 2 + 2 * T, cz)
        vmem = pltpu.VMEM
        call = pl.pallas_call(
            functools.partial(kernel, sizes),
            out_shape=jax.ShapeDtypeStruct(source.shape, F32),
            in_specs=[pl.BlockSpec(memory_space=pltpu.HBM)] * 2,
            out_specs=pl.BlockSpec(memory_space=vmem),
            scratch_shapes=[
                vmem((2,) + fine, F32),
                vmem((cy, cz), F32),
                vmem((3, cy + 2 * T, cz), F32),
                vmem((3, cy + 2 * T, cz), F32),
                vmem(fine, F32),
                vmem(fine, F32),
                vmem(fine, F32),
                vmem(fine, F32),
                vmem(fine, F32),
                vmem(fine, F32),
                vmem(fine, F32),
                vmem((2, cx // 2, cy + 2 * T, cz), F32),
                vmem((2, cx + 4, 2 * mid[1], cz), F32),
                vmem((cx // 4, mid[1], cz), F32),
                vmem((3,) + mid, F32),
                vmem((3, cy // 2, cz), F32),
                vmem((3, 3) + mid[1:], F32),
                vmem((3, 3) + mid[1:], F32),
                vmem((2, 2, cx // 2, cy // 2, cz), F32),
                pltpu.SemaphoreType.DMA((copies,)),
                pltpu.SemaphoreType.DMA((copies,)),
                pltpu.SemaphoreType.DMA((2,)),
            ],
            compiler_params=pltpu.CompilerParams(
                collective_id=0, has_side_effects=True, vmem_limit_bytes=48 * 2**20
            ),
        )
        return call(source, conductivity)

    return jax.shard_map(
        local, mesh=mesh, in_specs=(spec, spec), out_specs=spec, check_vma=False
    )
```

```python
import functools
import math

import jax
import jax.numpy as jnp
from jax import lax
from jax.experimental import pallas as pl
from jax.experimental.pallas import tpu as pltpu
from jax.sharding import PartitionSpec as P

spectrum_top = 1.9
spectrum_low = 0.475
omega_first = 1.0 / (
    (spectrum_top + spectrum_low) / 2 + (spectrum_top - spectrum_low) / 2 * math.cos(math.pi / 4)
)
omega_second = 1.0 / (
    (spectrum_top + spectrum_low) / 2
    + (spectrum_top - spectrum_low) / 2 * math.cos(3 * math.pi / 4)
)
F32 = jnp.float32
MESH = pl.DeviceIdType.MESH
H = 4
T = 8


def iota(shape, dim):
    return lax.broadcasted_iota(jnp.int32, shape, dim)


def parts(values):
    high = values.astype(jnp.bfloat16)
    rest = values - high.astype(F32)
    middle = rest.astype(jnp.bfloat16)
    return [high, middle, (rest - middle.astype(F32)).astype(jnp.bfloat16)]


def times(values, weights):
    size = values.shape[0]
    result = jnp.dot(
        jnp.concatenate(parts(values), axis=0),
        weights.astype(jnp.bfloat16),
        preferred_element_type=F32,
    )
    return result[:size] + (result[size : 2 * size] + result[2 * size :])


def weigh(weights, values):
    return jnp.dot(
        jnp.concatenate([weights.astype(jnp.bfloat16)] * 3, axis=1),
        jnp.concatenate(parts(values), axis=0),
        preferred_element_type=F32,
    )


def ring(index, size, cut):
    return jnp.where(index >= cut, index - size, index)


def restrict_weight(diff):
    side = (diff == -1) | (diff == 2)
    centre = (diff == 0) | (diff == 1)
    return jnp.where(centre, 0.375, jnp.where(side, 0.125, 0.0)).astype(F32)


def mean_weight(diff):
    return jnp.where((diff == 0) | (diff == 1), 0.5, 0.0).astype(F32)


def interpolate_weight(fine, coarse):
    base = (fine + 64) // 2 - 32
    other = base + jnp.where((fine + 64) % 2 == 0, -1, 1)
    return jnp.where(coarse == base, 0.75, jnp.where(coarse == other, 0.25, 0.0)).astype(F32)


def shift(values, axis, amount):
    size = values.shape[axis]
    return pltpu.roll(values, (-amount) % size, axis)


def span(way, extent, halo):
    if way == 0:
        return pl.ds(halo, extent), pl.ds(halo, extent)
    if way > 0:
        return pl.ds(extent, halo), pl.ds(0, halo)
    return pl.ds(halo, halo), pl.ds(halo + extent, halo)


ways = (0, 1, -1)
others = [(a, b, c) for c in ways for b in ways for a in ways if (a, b, c) != (0, 0, 0)]
mates = [(a, b, c) for a in (0, 1) for b in (0, 1) for c in (0, 1) if (a, b, c) != (0, 0, 0)]
axes = ("gx", "gy", "gz")
copies = 4 * len(others) + 2 * len(mates)


def kernel(
    sizes, s_ref, k_ref, out_ref,
    ks, pk, qa, qb, wx, wy, wz, iv, ua, ub, left, rs, fs, cs,
    mid, mp, ma, mb, cg, send_sem, recv_sem, load_sem,
):
    cx, cy, cz_ = s_ref.shape
    hx, hy, hz = cx // 2, cy // 2, cz_ // 2
    qx, qy, qz = cx // 4, cy // 4, cz_ // 4
    ex, ey, ez = ks.shape[1:]
    mx, my, mz = mid.shape[1:]
    pos = {axis: lax.axis_index(axis) for axis in axes}
    used = [0]

    def has(offset, sign):
        here = None
        for axis, way in zip(axes, offset):
            if way != 0:
                good = pos[axis] < sizes[axis] - 1 if way * sign > 0 else pos[axis] > 0
                here = good if here is None else here & good
        return here

    def make(offset, src, dst, number):
        return pltpu.make_async_remote_copy(
            src_ref=src, dst_ref=dst, send_sem=send_sem.at[number], recv_sem=recv_sem.at[number],
            device_id={axis: pos[axis] + way for axis, way in zip(axes, offset)},
            device_id_type=MESH,
        )

    def start(items):
        started = []
        for offset, src, dst in items:
            number = used[0]
            used[0] += 1
            started.append((offset, src, dst, number))

            @pl.when(has(offset, 1))
            def _():
                make(offset, src, dst, number).start()

        return started

    def finish_recv(started, wanted=lambda offset: True):
        for offset, src, dst, number in started:
            if not wanted(offset):
                continue

            @pl.when(has(offset, -1))
            def _():
                make(offset, src, dst, number).wait_recv()

    def finish_send(started):
        for offset, src, dst, number in started:

            @pl.when(has(offset, 1))
            def _():
                make(offset, src, dst, number).wait_send()

    loads = []
    for f, ref in enumerate((k_ref, s_ref)):
        own = ks.at[f, pl.ds(H, cx), pl.ds(T, cy), pl.ds(0, cz_)]
        loads.append(pltpu.make_async_copy(ref, own, load_sem.at[f]))
        loads[f].start()
    for f in range(2):
        for i in range(ex):
            if H <= i < H + cx:
                ks[f, i, 0:T, 0:cz_] = jnp.zeros((T, cz_), F32)
                ks[f, i, T + cy : ey, 0:cz_] = jnp.zeros((T, cz_), F32)
            else:
                ks[f, i, :, 0:cz_] = jnp.zeros((ey, cz_), F32)
    qa[...] = jnp.zeros(qa.shape, F32)
    qb[...] = jnp.zeros(qb.shape, F32)
    mid[...] = jnp.zeros(mid.shape, F32)
    ma[...] = jnp.zeros(ma.shape, F32)
    mb[...] = jnp.zeros(mb.shape, F32)
    barrier = pltpu.get_barrier_semaphore()
    count = 0
    for offset in others:
        here = has(offset, 1)
        count = count + here.astype(jnp.int32)

        @pl.when(here)
        def _():
            pl.semaphore_signal(
                barrier, inc=1,
                device_id={axis: pos[axis] + way for axis, way in zip(axes, offset)},
                device_id_type=MESH,
            )

    group = iota((cy, cz_), 1) // (2 * H)
    packed = jnp.zeros((cy, cz_), F32)
    for f in range(2):
        loads[f].wait()
        for p in range(cx):
            g = f * cx + p
            own = ks[f, H + p, T : T + cy, 0:cz_]
            packed = jnp.where(group == g, shift(own, 1, -(H + 2 * H * g)), packed)
    pk[...] = packed
    pl.semaphore_wait(barrier, count)

    main = pl.ds(0, cz_)
    items = []
    for offset in others:
        dx, dy, dz = offset
        xs, xd = span(dx, cx, H)
        ys, yd = span(dy, cy, T)
        if dz == 0:
            items.append((offset, ks.at[:, xs, ys, main], ks.at[:, xd, yd, main]))
        else:
            target = qa if dz > 0 else qb
            rows = pl.ds(ys.start - T, ys.size)
            items.append((offset, pk.at[rows], target.at[1 - dx, yd]))
    fine_round = start(items)

    mgroup = iota((hy, mz), 1) // H

    def middle_start(f):
        packed = jnp.zeros((hy, mz), F32)
        for p in range(hx):
            own = mid[f, hx + p, T : T + hy, :]
            packed = jnp.where(mgroup == 2 * p, shift(own, 1, hz - H - 2 * H * p), packed)
            packed = jnp.where(mgroup == 2 * p + 1, shift(own, 1, -(2 * H * p + H)), packed)
        mp[f] = packed
        items = []
        for offset in others:
            dx, dy, dz = offset
            xs, xd = span(dx, hx, hx)
            ys, yd = span(dy, hy, T)
            if dz == 0:
                items.append((offset, mid.at[f, xs, ys], mid.at[f, xd, yd]))
            else:
                target = ma if dz > 0 else mb
                rows = pl.ds(ys.start - T, ys.size)
                items.append((offset, mp.at[f, rows], target.at[f, 1 - dx, yd]))
        return start(items)

    mlane = iota((my, mz), 1)

    def middle_finish(f, started):
        finish_recv(started)
        planes = []
        for i in range(mx):
            block, p = i // hx, i % hx
            right = shift(mb[f, block], 1, 2 * H * p + H - hz)
            left = shift(ma[f, block], 1, 2 * H * p - (mz - H))
            side = jnp.where(mlane < (hz + mz) // 2, right, left)
            planes.append(jnp.where(mlane < hz, mid[f, i], side)[None])
        return jnp.concatenate(planes, axis=0)

    px, py, pz = (pos[axis] % 2 for axis in axes)
    here = pl.ds(px * qx, qx)
    line = pl.ds(pl.multiple_of(py * qy, qy), qy)

    def gather_make(f, flips, number):
        return pltpu.make_async_remote_copy(
            src_ref=cg.at[f, 0, here, line], dst_ref=cg.at[f, flips[2], here, line],
            send_sem=send_sem.at[number], recv_sem=recv_sem.at[number],
            device_id={
                axis: pos[axis] + (1 - 2 * (pos[axis] % 2)) * flip for axis, flip in zip(axes, flips)
            },
            device_id_type=MESH,
        )

    def gather_start(f):
        started = []
        for flips in mates:
            copy = gather_make(f, flips, used[0])
            used[0] += 1
            copy.start()
            started.append(copy)
        return started

    lz = iota((cz_, mz), 0) - 2 * iota((cz_, mz), 1)
    mean_z = jnp.where(iota((cz_, mz), 1) < hz, mean_weight(lz), 0.0)
    for i in range(hx):
        own = [ks[0, H + 2 * i + j, T : T + cy, 0:cz_] for j in range(2)]
        rs[0, i, T : T + cy, :] = (own[0] + own[1]) * 0.5
    means = [
        (rs[0, i, pl.ds(T, hy, stride=2), :] + rs[0, i, pl.ds(T + 1, hy, stride=2), :]) * 0.5
        for i in range(hx)
    ]
    means = times(jnp.concatenate(means, axis=0), mean_z)
    for i in range(hx):
        mid[0, hx + i, T : T + hy, :] = means[i * hy : (i + 1) * hy]
    coeff_round = middle_start(0)

    cj = iota((mz, mz), 1) - pz * qz
    clz = ring(iota((mz, mz), 0), mz, (hz + mz) // 2) - 2 * cj
    ckeep = (cj >= 0) & (cj < qz)
    to_coarse_z = jnp.where(ckeep, restrict_weight(clz), 0.0)
    cmean_z = jnp.where(ckeep, mean_weight(clz), 0.0)
    for i in range(qx):
        own_rows = [mid[0, hx + 2 * i + j, T : T + hy, :] for j in range(2)]
        cs[i, T : T + hy, :] = (own_rows[0] + own_rows[1]) * 0.5
    means = [
        (cs[i, pl.ds(T, qy, stride=2), :] + cs[i, pl.ds(T + 1, qy, stride=2), :]) * 0.5
        for i in range(qx)
    ]
    means = times(jnp.concatenate(means, axis=0), cmean_z)
    for i in range(qx):
        cg[0, 0, px * qx + i, line, :] = means[i * qy : (i + 1) * qy]
    gather_coeff = gather_start(0)

    r = iota((ey, ez), 0) - T + pos["gy"] * cy
    local_z = ring(iota((ey, ez), 1), ez, ez - cz_ // 2)
    z = local_z + pos["gz"] * cz_
    fine_in = (r >= 0) & (r < cy * sizes["gy"]) & (z >= 0) & (z < cz_ * sizes["gz"])
    fine_in = fine_in & (local_z >= -H) & (local_z < cz_ + H)

    def plane_in(i):
        x = i - H + pos["gx"] * cx
        return (x >= 0) & (x < cx * sizes["gx"])

    lz = ring(iota((ez, mz), 0), ez, ez - cz_ // 2) - 2 * iota((ez, mz), 1)
    to_middle_z = jnp.where(iota((ez, mz), 1) < hz, restrict_weight(lz), 0.0)

    mr = iota((mx, my, mz), 1) - T + pos["gy"] * hy
    mlz = ring(iota((mx, my, mz), 2), mz, (hz + mz) // 2)
    mzz = mlz + pos["gz"] * hz
    mxx = iota((mx, my, mz), 0) - hx + pos["gx"] * hx
    middle_in = (
        (mr >= 0) & (mr < hy * sizes["gy"]) & (mzz >= 0) & (mzz < hz * sizes["gz"])
        & (mxx >= 0) & (mxx < hx * sizes["gx"]) & (mlz >= -H) & (mlz < hz + H)
    )

    jj = iota((mz, mz), 1)
    back_z = interpolate_weight(jj + pz * hz, iota((mz, mz), 0))
    back_z = jnp.where((jj < hz) & (iota((mz, mz), 0) < 2 * qz), back_z, 0.0)
    shape = (hx * hy, 4 * qx * qy)
    fine_i, coarse_i = iota(shape, 0), iota(shape, 1)
    back_xy = interpolate_weight(fine_i // hy + px * hx, coarse_i // (2 * qy)) * interpolate_weight(
        fine_i % hy + py * hy, coarse_i % (2 * qy)
    )
    fine_lane = ring(iota((mz, ez), 1), ez, ez - cz_ // 2)
    middle_lane = ring(iota((mz, ez), 0), mz, (hz + mz) // 2)
    wide = (fine_lane >= -H) & (fine_lane < cz_ + H)
    to_fine_z = jnp.where(wide, interpolate_weight(fine_lane, middle_lane), 0.0)

    lane = iota((ey, cz_), 1)

    def unpack(block):
        merged = jnp.where(lane % (2 * H) < H, qa[block], qb[block])
        for i in range(ex):
            if (i - H) // cx + 1 == block:
                for f in range(2):
                    p = (i - H) % cx
                    ks[f, i, :, cz_:ez] = shift(merged, 1, H + 2 * H * (f * cx + p))

    def weights(i, carry):
        k = ks[0, i]
        after = 0.5 * (k + ks[0, i + 1])
        a = 0.5 * (k + shift(k, 0, 1))
        b = 0.5 * (k + shift(k, 1, 1))
        diag = (wx[i - 1] + after) + (a + shift(a, 0, -1)) + (b + shift(b, 1, -1))
        wx[i] = after
        wy[i] = a
        wz[i] = b
        inverse = jnp.where(fine_in & plane_in(i), 1.0 / diag, 0.0)
        iv[i] = inverse
        ua[i] = omega_first * ks[1, i] * inverse
        return carry

    def around(u, i):
        v = u[i]
        a, b = wy[i], wz[i]
        total = wx[i] * u[i + 1] + wx[i - 1] * u[i - 1]
        total = total + (a * shift(v, 0, 1) + shift(a * v, 0, -1))
        total = total + (b * shift(v, 1, 1) + shift(b * v, 1, -1))
        return v, total

    def fine_sweep(u, i, omega):
        v, total = around(u, i)
        return (1.0 - omega) * v + omega * (ks[1, i] + total) * iv[i]

    def pre(i, carry):
        ub[i] = fine_sweep(ua, i, omega_second)
        return carry


    def leftover(i, carry):
        v, total = around(ub, i)
        inverse = iv[i]
        diag = wx[i] + wx[i - 1] + (wy[i] + shift(wy[i], 0, -1)) + (wz[i] + shift(wz[i], 1, -1))
        left[i] = jnp.where(inverse > 0.0, ks[1, i] - diag * v + total, 0.0)
        return carry

    def run(low, high, body):
        lax.fori_loop(low, high, body, 0, unroll=2)

    last_own = H + cx - 1
    finish_recv(fine_round, lambda offset: offset[0] == 0)
    unpack(1)
    wx[H] = 0.5 * (ks[0, H] + ks[0, H + 1])
    run(H + 1, last_own, weights)
    run(H + 2, last_own - 1, pre)
    run(H + 3, last_own - 2, leftover)
    finish_recv(fine_round, lambda offset: offset[0] != 0)
    unpack(0)
    unpack(2)
    wx[0] = 0.5 * (ks[0, 0] + ks[0, 1])
    run(1, H + 1, weights)
    run(last_own, ex - 1, weights)
    run(2, H + 2, pre)
    run(last_own - 1, ex - 2, pre)
    run(3, H + 3, leftover)
    run(last_own - 2, ex - 3, leftover)

    def restrict_rows(take):
        side = take(T - 1) + take(T + 2)
        return side * 0.125 + (take(T) + take(T + 1)) * 0.375

    pieces = []
    for i in range(hx):
        c = H + 2 * i
        mixed = (left[c - 1] + left[c + 2]) * 0.5 + (left[c] + left[c + 1]) * 1.5
        rs[0, i] = mixed[:, :cz_]
        rs[1, i] = mixed[:, cz_:]
        halves = [
            restrict_rows(lambda first: rs[t, i, pl.ds(first, hy, stride=2), :]) for t in range(2)
        ]
        pieces.append(jnp.concatenate(halves, axis=1))
    rhs = times(jnp.concatenate(pieces, axis=0), to_middle_z)
    for i in range(hx):
        mid[1, hx + i, T : T + hy, :] = rhs[i * hy : (i + 1) * hy]
    rhs_round = middle_start(1)

    def up(values):
        return jnp.concatenate([values[1:], values[:1]], axis=0)

    def down(values):
        return jnp.concatenate([values[-1:], values[:-1]], axis=0)

    def faces(k):
        return 0.5 * (k + up(k)), 0.5 * (k + shift(k, 1, 1)), 0.5 * (k + shift(k, 2, 1))

    def diagonal(w):
        return (w[0] + down(w[0])) + (w[1] + shift(w[1], 1, -1)) + (w[2] + shift(w[2], 2, -1))

    def neighbours(w, v):
        total = w[0] * up(v) + down(w[0] * v)
        total = total + (w[1] * shift(v, 1, 1) + shift(w[1] * v, 1, -1))
        return total + (w[2] * shift(v, 2, 1) + shift(w[2] * v, 2, -1))

    def sweep(w, inverse, v, f, omega):
        return (1.0 - omega) * v + omega * (f + neighbours(w, v)) * inverse

    mk = middle_finish(0, coeff_round)
    mw = faces(mk)
    mdiag = diagonal(mw)
    miv = jnp.where(middle_in, 1.0 / mdiag, 0.0)

    for copy in gather_coeff:
        copy.wait_recv()
    ck = cg[0, 0] + cg[0, 1]
    cshape = ck.shape
    row = iota(cshape, 1)
    plane = iota(cshape, 0)
    box_in = iota(cshape, 2) < 2 * qz
    nx, ny = 2 * qx, 2 * qy
    cw = faces(ck)
    half = 0.5 * ck
    cwx = jnp.where(plane < nx - 1, cw[0], 0.0)
    cwy = jnp.where(row < ny - 1, cw[1], 0.0)
    cw = (cwx, cwy, cw[2])
    cdiag = diagonal(cw)
    cdiag = cdiag + jnp.where(plane == 0, half, 0.0) + jnp.where(plane == nx - 1, half, 0.0)
    cdiag = cdiag + jnp.where(row == 0, half, 0.0) + jnp.where(row == ny - 1, half, 0.0)
    civ = jnp.where(box_in, 1.0 / cdiag, 0.0)

    finish_send(fine_round)
    finish_send(coeff_round)
    for copy in gather_coeff:
        copy.wait_send()
    mf = middle_finish(1, rhs_round)
    m1 = omega_first * mf * miv
    m2 = sweep(mw, miv, m1, mf, omega_second)
    mleft = jnp.where(middle_in, mf - mdiag * m2 + neighbours(mw, m2), 0.0)

    pieces = []
    for i in range(qx):
        c = hx + 2 * i
        cs[i] = (mleft[c - 1] + mleft[c + 2]) * 0.5 + (mleft[c] + mleft[c + 1]) * 1.5
        pieces.append(restrict_rows(lambda first: cs[i, pl.ds(first, qy, stride=2), :]))
    rhs = times(jnp.concatenate(pieces, axis=0), to_coarse_z)
    for i in range(qx):
        cg[1, 0, px * qx + i, line, :] = rhs[i * qy : (i + 1) * qy]
    gather_rhs = gather_start(1)
    finish_send(rhs_round)
    for copy in gather_rhs:
        copy.wait_recv()

    cf = cg[1, 0] + cg[1, 1]
    c1 = omega_first * cf * civ
    c2 = sweep(cw, civ, c1, cf, omega_second)
    flat = c2.reshape(nx * ny, mz)
    correction = weigh(back_xy, times(flat, back_z))
    for i in range(hx):
        fixed = m2[hx + i, T : T + hy, :] + correction[i * hy : (i + 1) * hy]
        mid[2, hx + i, T : T + hy, :] = fixed
    last_round = middle_start(2)
    for copy in gather_rhs:
        copy.wait_send()
    m3 = middle_finish(2, last_round)
    m4 = sweep(mw, miv, m3, mf, omega_first)
    m5 = sweep(mw, miv, m4, mf, omega_second)

    low = hx - 2
    spread = times(m5[low : 2 * hx + 2].reshape((hx + 4) * my, mz), to_fine_z)
    for i in range(2, ex - 2):
        c = (i - H + 64) // 2 - 32 + hx - low
        other = c - 1 if i % 2 == 0 else c + 1
        mixed = 0.75 * spread[c * my : (c + 1) * my] + 0.25 * spread[other * my : (other + 1) * my]
        near = 0.75 * mixed
        even = near + 0.25 * shift(mixed, 0, -1)
        odd = near + 0.25 * shift(mixed, 0, 1)
        for t in range(2):
            lanes = slice(t * cz_, (t + 1) * cz_)
            fs[t, i - 2, pl.ds(0, my, stride=2), :] = even[:, lanes]
            fs[t, i - 2, pl.ds(1, my, stride=2), :] = odd[:, lanes]
    for i in range(2, ex - 2):
        rows = slice(2 * T - T, 2 * T - T + ey)
        fresh = jnp.concatenate([fs[0, i - 2, rows, :], fs[1, i - 2, rows, :]], axis=1)
        ua[i] = jnp.where(fine_in & plane_in(i), ub[i] + fresh, 0.0)

    def post(i, carry):
        ub[i] = fine_sweep(ua, i, omega_first)
        return carry

    lax.fori_loop(3, ex - 3, post, 0, unroll=2)

    def last(i, carry):
        out_ref[i - H] = fine_sweep(ub, i, omega_second)[T : T + cy, 0:cz_]
        return carry

    lax.fori_loop(H, H + cx, last, 0, unroll=2)
    finish_send(last_round)


def solution(mesh):
    sizes = {axis: mesh.shape[axis] for axis in mesh.axis_names}
    spec = P("gx", "gy", "gz")

    def local(source, conductivity):
        cx, cy, cz = source.shape
        fine = (cx + 2 * H, cy + 2 * T, 2 * cz)
        mid = (cx // 2 * 3, cy // 2 + 2 * T, cz)
        vmem = pltpu.VMEM
        call = pl.pallas_call(
            functools.partial(kernel, sizes),
            out_shape=jax.ShapeDtypeStruct(source.shape, F32),
            in_specs=[pl.BlockSpec(memory_space=pltpu.HBM)] * 2,
            out_specs=pl.BlockSpec(memory_space=vmem),
            scratch_shapes=[
                vmem((2,) + fine, F32),
                vmem((cy, cz), F32),
                vmem((3, cy + 2 * T, cz), F32),
                vmem((3, cy + 2 * T, cz), F32),
                vmem(fine, F32),
                vmem(fine, F32),
                vmem(fine, F32),
                vmem(fine, F32),
                vmem(fine, F32),
                vmem(fine, F32),
                vmem(fine, F32),
                vmem((2, cx // 2, cy + 2 * T, cz), F32),
                vmem((2, cx + 4, 2 * mid[1], cz), F32),
                vmem((cx // 4, mid[1], cz), F32),
                vmem((3,) + mid, F32),
                vmem((3, cy // 2, cz), F32),
                vmem((3, 3) + mid[1:], F32),
                vmem((3, 3) + mid[1:], F32),
                vmem((2, 2, cx // 2, cy // 2, cz), F32),
                pltpu.SemaphoreType.DMA((copies,)),
                pltpu.SemaphoreType.DMA((copies,)),
                pltpu.SemaphoreType.DMA((2,)),
            ],
            compiler_params=pltpu.CompilerParams(
                collective_id=0, has_side_effects=True, vmem_limit_bytes=48 * 2**20
            ),
        )
        return call(*(pltpu.with_memory_space_constraint(v, pltpu.HBM) for v in (source, conductivity)))

    return jax.shard_map(
        local, mesh=mesh, in_specs=(spec, spec), out_specs=spec, check_vma=False
    )
```

```python
import functools
import math

import jax
import jax.numpy as jnp
from jax import lax
from jax.experimental import pallas as pl
from jax.experimental.pallas import tpu as pltpu
from jax.sharding import PartitionSpec as P

spectrum_top = 1.9
spectrum_low = 0.475
omega_first = 1.0 / (
    (spectrum_top + spectrum_low) / 2 + (spectrum_top - spectrum_low) / 2 * math.cos(math.pi / 4)
)
omega_second = 1.0 / (
    (spectrum_top + spectrum_low) / 2
    + (spectrum_top - spectrum_low) / 2 * math.cos(3 * math.pi / 4)
)
F32 = jnp.float32
MESH = pl.DeviceIdType.MESH
H = 4
T = 8


def iota(shape, dim):
    return lax.broadcasted_iota(jnp.int32, shape, dim)


def parts(values):
    high = values.astype(jnp.bfloat16)
    rest = values - high.astype(F32)
    middle = rest.astype(jnp.bfloat16)
    return [high, middle, (rest - middle.astype(F32)).astype(jnp.bfloat16)]


def times(values, weights):
    size = values.shape[0]
    result = jnp.dot(
        jnp.concatenate(parts(values), axis=0),
        weights.astype(jnp.bfloat16),
        preferred_element_type=F32,
    )
    return result[:size] + (result[size : 2 * size] + result[2 * size :])


def weigh(weights, values):
    return jnp.dot(
        jnp.concatenate([weights.astype(jnp.bfloat16)] * 3, axis=1),
        jnp.concatenate(parts(values), axis=0),
        preferred_element_type=F32,
    )


def ring(index, size, cut):
    return jnp.where(index >= cut, index - size, index)


def restrict_weight(diff):
    side = (diff == -1) | (diff == 2)
    centre = (diff == 0) | (diff == 1)
    return jnp.where(centre, 0.375, jnp.where(side, 0.125, 0.0)).astype(F32)


def mean_weight(diff):
    return jnp.where((diff == 0) | (diff == 1), 0.5, 0.0).astype(F32)


def interpolate_weight(fine, coarse):
    base = (fine + 64) // 2 - 32
    other = base + jnp.where((fine + 64) % 2 == 0, -1, 1)
    return jnp.where(coarse == base, 0.75, jnp.where(coarse == other, 0.25, 0.0)).astype(F32)


def shift(values, axis, amount):
    size = values.shape[axis]
    return pltpu.roll(values, (-amount) % size, axis)


def span(way, extent, halo):
    if way == 0:
        return pl.ds(halo, extent), pl.ds(halo, extent)
    if way > 0:
        return pl.ds(extent, halo), pl.ds(0, halo)
    return pl.ds(halo, halo), pl.ds(halo + extent, halo)


ways = (0, 1, -1)
others = [(a, b, c) for c in ways for b in ways for a in ways if (a, b, c) != (0, 0, 0)]
mates = [(a, b, c) for a in (0, 1) for b in (0, 1) for c in (0, 1) if (a, b, c) != (0, 0, 0)]
axes = ("gx", "gy", "gz")
copies = 4 * len(others) + 2 * len(mates)


def kernel(
    sizes, s_ref, k_ref, out_ref,
    ks, pk, qa, qb, wx, wy, wz, dg, iv, ua, ub, left, rs, fs, cs,
    mk, mf, mwx, mwy, mwz, mdg, miv, va, vb, vc,
    mid, mp, ma, mb, cg, send_sem, recv_sem, load_sem,
):
    cx, cy, cz_ = s_ref.shape
    hx, hy, hz = cx // 2, cy // 2, cz_ // 2
    qx, qy, qz = cx // 4, cy // 4, cz_ // 4
    ex, ey, ez = ks.shape[1:]
    mx, my, mz = mid.shape[1:]
    pos = {axis: lax.axis_index(axis) for axis in axes}
    used = [0]

    def has(offset, sign):
        here = None
        for axis, way in zip(axes, offset):
            if way != 0:
                good = pos[axis] < sizes[axis] - 1 if way * sign > 0 else pos[axis] > 0
                here = good if here is None else here & good
        return here

    def make(offset, src, dst, number):
        return pltpu.make_async_remote_copy(
            src_ref=src, dst_ref=dst, send_sem=send_sem.at[number], recv_sem=recv_sem.at[number],
            device_id={axis: pos[axis] + way for axis, way in zip(axes, offset)},
            device_id_type=MESH,
        )

    def start(items):
        started = []
        for offset, src, dst in items:
            number = used[0]
            used[0] += 1
            started.append((offset, src, dst, number))

            @pl.when(has(offset, 1))
            def _():
                make(offset, src, dst, number).start()

        return started

    def finish_recv(started, wanted=lambda offset: True):
        for offset, src, dst, number in started:
            if not wanted(offset):
                continue

            @pl.when(has(offset, -1))
            def _():
                make(offset, src, dst, number).wait_recv()

    def finish_send(started):
        for offset, src, dst, number in started:

            @pl.when(has(offset, 1))
            def _():
                make(offset, src, dst, number).wait_send()

    loads = []
    for f, ref in enumerate((k_ref, s_ref)):
        own = ks.at[f, pl.ds(H, cx), pl.ds(T, cy), pl.ds(0, cz_)]
        loads.append(pltpu.make_async_copy(ref, own, load_sem.at[f]))
        loads[f].start()
    for f in range(2):
        for i in range(ex):
            if H <= i < H + cx:
                ks[f, i, 0:T, 0:cz_] = jnp.zeros((T, cz_), F32)
                ks[f, i, T + cy : ey, 0:cz_] = jnp.zeros((T, cz_), F32)
            else:
                ks[f, i, :, 0:cz_] = jnp.zeros((ey, cz_), F32)
    qa[...] = jnp.zeros(qa.shape, F32)
    qb[...] = jnp.zeros(qb.shape, F32)
    mid[...] = jnp.zeros(mid.shape, F32)
    ma[...] = jnp.zeros(ma.shape, F32)
    mb[...] = jnp.zeros(mb.shape, F32)
    barrier = pltpu.get_barrier_semaphore()
    count = 0
    for offset in others:
        here = has(offset, 1)
        count = count + here.astype(jnp.int32)

        @pl.when(here)
        def _():
            pl.semaphore_signal(
                barrier, inc=1,
                device_id={axis: pos[axis] + way for axis, way in zip(axes, offset)},
                device_id_type=MESH,
            )

    group = iota((cy, cz_), 1) // (2 * H)
    packed = jnp.zeros((cy, cz_), F32)
    for f in range(2):
        loads[f].wait()
        for p in range(cx):
            g = f * cx + p
            own = ks[f, H + p, T : T + cy, 0:cz_]
            packed = jnp.where(group == g, shift(own, 1, -(H + 2 * H * g)), packed)
    pk[...] = packed
    pl.semaphore_wait(barrier, count)

    main = pl.ds(0, cz_)
    items = []
    for offset in others:
        dx, dy, dz = offset
        xs, xd = span(dx, cx, H)
        ys, yd = span(dy, cy, T)
        if dz == 0:
            items.append((offset, ks.at[:, xs, ys, main], ks.at[:, xd, yd, main]))
        else:
            target = qa if dz > 0 else qb
            rows = pl.ds(ys.start - T, ys.size)
            items.append((offset, pk.at[rows], target.at[1 - dx, yd]))
    fine_round = start(items)

    mgroup = iota((hy, mz), 1) // H

    def middle_start(f):
        packed = jnp.zeros((hy, mz), F32)
        for p in range(hx):
            own = mid[f, hx + p, T : T + hy, :]
            packed = jnp.where(mgroup == 2 * p, shift(own, 1, hz - H - 2 * H * p), packed)
            packed = jnp.where(mgroup == 2 * p + 1, shift(own, 1, -(2 * H * p + H)), packed)
        mp[f] = packed
        items = []
        for offset in others:
            dx, dy, dz = offset
            xs, xd = span(dx, hx, hx)
            ys, yd = span(dy, hy, T)
            if dz == 0:
                items.append((offset, mid.at[f, xs, ys], mid.at[f, xd, yd]))
            else:
                target = ma if dz > 0 else mb
                rows = pl.ds(ys.start - T, ys.size)
                items.append((offset, mp.at[f, rows], target.at[f, 1 - dx, yd]))
        return start(items)

    mlane = iota((my, mz), 1)

    def middle_finish(f, started, put):
        finish_recv(started)
        for i in range(mx):
            block, p = i // hx, i % hx
            right = shift(mb[f, block], 1, 2 * H * p + H - hz)
            left_side = shift(ma[f, block], 1, 2 * H * p - (mz - H))
            side = jnp.where(mlane < (hz + mz) // 2, right, left_side)
            put(i, jnp.where(mlane < hz, mid[f, i], side))

    px, py, pz = (pos[axis] % 2 for axis in axes)
    here = pl.ds(px * qx, qx)
    line = pl.ds(pl.multiple_of(py * qy, qy), qy)

    def gather_make(f, flips, number):
        return pltpu.make_async_remote_copy(
            src_ref=cg.at[f, 0, here, line], dst_ref=cg.at[f, flips[2], here, line],
            send_sem=send_sem.at[number], recv_sem=recv_sem.at[number],
            device_id={
                axis: pos[axis] + (1 - 2 * (pos[axis] % 2)) * flip for axis, flip in zip(axes, flips)
            },
            device_id_type=MESH,
        )

    def gather_start(f):
        started = []
        for flips in mates:
            copy = gather_make(f, flips, used[0])
            used[0] += 1
            copy.start()
            started.append(copy)
        return started

    lz = iota((cz_, mz), 0) - 2 * iota((cz_, mz), 1)
    mean_z = jnp.where(iota((cz_, mz), 1) < hz, mean_weight(lz), 0.0)
    for i in range(hx):
        own = [ks[0, H + 2 * i + j, T : T + cy, 0:cz_] for j in range(2)]
        rs[0, i, T : T + cy, :] = (own[0] + own[1]) * 0.5
    means = [
        (rs[0, i, pl.ds(T, hy, stride=2), :] + rs[0, i, pl.ds(T + 1, hy, stride=2), :]) * 0.5
        for i in range(hx)
    ]
    means = times(jnp.concatenate(means, axis=0), mean_z)
    for i in range(hx):
        mid[0, hx + i, T : T + hy, :] = means[i * hy : (i + 1) * hy]
    coeff_round = middle_start(0)

    cj = iota((mz, mz), 1) - pz * qz
    clz = ring(iota((mz, mz), 0), mz, (hz + mz) // 2) - 2 * cj
    ckeep = (cj >= 0) & (cj < qz)
    to_coarse_z = jnp.where(ckeep, restrict_weight(clz), 0.0)
    cmean_z = jnp.where(ckeep, mean_weight(clz), 0.0)
    for i in range(qx):
        own_rows = [mid[0, hx + 2 * i + j, T : T + hy, :] for j in range(2)]
        cs[i, T : T + hy, :] = (own_rows[0] + own_rows[1]) * 0.5
    means = [
        (cs[i, pl.ds(T, qy, stride=2), :] + cs[i, pl.ds(T + 1, qy, stride=2), :]) * 0.5
        for i in range(qx)
    ]
    means = times(jnp.concatenate(means, axis=0), cmean_z)
    for i in range(qx):
        cg[0, 0, px * qx + i, line, :] = means[i * qy : (i + 1) * qy]
    gather_coeff = gather_start(0)

    r = iota((ey, ez), 0) - T + pos["gy"] * cy
    local_z = ring(iota((ey, ez), 1), ez, ez - cz_ // 2)
    z = local_z + pos["gz"] * cz_
    fine_in = (r >= 0) & (r < cy * sizes["gy"]) & (z >= 0) & (z < cz_ * sizes["gz"])
    fine_in = fine_in & (local_z >= -H) & (local_z < cz_ + H)

    def plane_in(i):
        x = i - H + pos["gx"] * cx
        return (x >= 0) & (x < cx * sizes["gx"])

    lz = ring(iota((ez, mz), 0), ez, ez - cz_ // 2) - 2 * iota((ez, mz), 1)
    to_middle_z = jnp.where(iota((ez, mz), 1) < hz, restrict_weight(lz), 0.0)

    mr = iota((my, mz), 0) - T + pos["gy"] * hy
    mlz = ring(iota((my, mz), 1), mz, (hz + mz) // 2)
    mzz = mlz + pos["gz"] * hz
    middle_in = (
        (mr >= 0) & (mr < hy * sizes["gy"]) & (mzz >= 0) & (mzz < hz * sizes["gz"])
        & (mlz >= -H) & (mlz < hz + H)
    )

    def middle_plane_in(i):
        x = i - hx + pos["gx"] * hx
        return (x >= 0) & (x < hx * sizes["gx"])

    jj = iota((mz, mz), 1)
    back_z = interpolate_weight(jj + pz * hz, iota((mz, mz), 0))
    back_z = jnp.where((jj < hz) & (iota((mz, mz), 0) < 2 * qz), back_z, 0.0)
    shape = (hx * hy, 4 * qx * qy)
    fine_i, coarse_i = iota(shape, 0), iota(shape, 1)
    back_xy = interpolate_weight(fine_i // hy + px * hx, coarse_i // (2 * qy)) * interpolate_weight(
        fine_i % hy + py * hy, coarse_i % (2 * qy)
    )
    fine_lane = ring(iota((mz, ez), 1), ez, ez - cz_ // 2)
    middle_lane = ring(iota((mz, ez), 0), mz, (hz + mz) // 2)
    wide = (fine_lane >= -H) & (fine_lane < cz_ + H)
    to_fine_z = jnp.where(wide, interpolate_weight(fine_lane, middle_lane), 0.0)

    lane = iota((ey, cz_), 1)

    def unpack(block):
        merged = jnp.where(lane % (2 * H) < H, qa[block], qb[block])
        for i in range(ex):
            if (i - H) // cx + 1 == block:
                for f in range(2):
                    p = (i - H) % cx
                    ks[f, i, :, cz_:ez] = shift(merged, 1, H + 2 * H * (f * cx + p))

    fine_w = (wx, wy, wz, dg, iv)
    middle_w = (mwx, mwy, mwz, mdg, miv)

    def set_weights(w, k_of, i, inside):
        ax, ay, az, diag_ref, inverse_ref = w
        k = k_of(i)
        after = 0.5 * (k + k_of(i + 1))
        a = 0.5 * (k + shift(k, 0, 1))
        b = 0.5 * (k + shift(k, 1, 1))
        diag = (ax[i - 1] + after) + (a + shift(a, 0, -1)) + (b + shift(b, 1, -1))
        ax[i] = after
        ay[i] = a
        az[i] = b
        diag_ref[i] = diag
        inverse = jnp.where(inside, 1.0 / diag, 0.0)
        inverse_ref[i] = inverse
        return inverse

    def around(w, u, i):
        v = u[i]
        a, b = w[1][i], w[2][i]
        total = w[0][i] * u[i + 1] + w[0][i - 1] * u[i - 1]
        total = total + (a * shift(v, 0, 1) + shift(a * v, 0, -1))
        total = total + (b * shift(v, 1, 1) + shift(b * v, 1, -1))
        return v, total

    def plane_sweep(w, f, u, i, omega):
        v, total = around(w, u, i)
        return (1.0 - omega) * v + omega * (f + total) * w[4][i]

    def plane_left(w, f, u, i):
        v, total = around(w, u, i)
        return jnp.where(w[4][i] > 0.0, f - w[3][i] * v + total, 0.0)

    def run(low, high, body):
        def step(i, carry):
            body(i)
            return carry

        lax.fori_loop(low, high, step, 0, unroll=2)

    def weights(i):
        inverse = set_weights(fine_w, lambda j: ks[0, j], i, fine_in & plane_in(i))
        ua[i] = omega_first * ks[1, i] * inverse

    def pre(i):
        ub[i] = plane_sweep(fine_w, ks[1, i], ua, i, omega_second)

    def leftover(i):
        left[i] = plane_left(fine_w, ks[1, i], ub, i)

    last_own = H + cx - 1
    finish_recv(fine_round, lambda offset: offset[0] == 0)
    unpack(1)
    wx[H] = 0.5 * (ks[0, H] + ks[0, H + 1])
    run(H + 1, last_own, weights)
    run(H + 2, last_own - 1, pre)
    run(H + 3, last_own - 2, leftover)
    finish_recv(fine_round, lambda offset: offset[0] != 0)
    unpack(0)
    unpack(2)
    wx[0] = 0.5 * (ks[0, 0] + ks[0, 1])
    run(1, H + 1, weights)
    run(last_own, ex - 1, weights)
    run(2, H + 2, pre)
    run(last_own - 1, ex - 2, pre)
    run(3, H + 3, leftover)
    run(last_own - 2, ex - 3, leftover)

    def restrict_rows(take):
        side = take(T - 1) + take(T + 2)
        return side * 0.125 + (take(T) + take(T + 1)) * 0.375

    pieces = []
    for i in range(hx):
        c = H + 2 * i
        mixed = (left[c - 1] + left[c + 2]) * 0.5 + (left[c] + left[c + 1]) * 1.5
        rs[0, i] = mixed[:, :cz_]
        rs[1, i] = mixed[:, cz_:]
        halves = [
            restrict_rows(lambda first: rs[t, i, pl.ds(first, hy, stride=2), :]) for t in range(2)
        ]
        pieces.append(jnp.concatenate(halves, axis=1))
    rhs = times(jnp.concatenate(pieces, axis=0), to_middle_z)
    for i in range(hx):
        mid[1, hx + i, T : T + hy, :] = rhs[i * hy : (i + 1) * hy]
    rhs_round = middle_start(1)

    def up(values):
        return jnp.concatenate([values[1:], values[:1]], axis=0)

    def down(values):
        return jnp.concatenate([values[-1:], values[:-1]], axis=0)

    def faces(k):
        return 0.5 * (k + up(k)), 0.5 * (k + shift(k, 1, 1)), 0.5 * (k + shift(k, 2, 1))

    def diagonal(w):
        return (w[0] + down(w[0])) + (w[1] + shift(w[1], 1, -1)) + (w[2] + shift(w[2], 2, -1))

    def neighbours(w, v):
        total = w[0] * up(v) + down(w[0] * v)
        total = total + (w[1] * shift(v, 1, 1) + shift(w[1] * v, 1, -1))
        return total + (w[2] * shift(v, 2, 1) + shift(w[2] * v, 2, -1))

    def sweep(w, inverse, v, f, omega):
        return (1.0 - omega) * v + omega * (f + neighbours(w, v)) * inverse

    def put_coeff(i, values):
        mk[i] = values

    middle_finish(0, coeff_round, put_coeff)
    mwx[0] = 0.5 * (mk[0] + mk[1])

    def middle_weights(i):
        set_weights(middle_w, lambda j: mk[j], i, middle_in & middle_plane_in(i))

    run(1, mx - 1, middle_weights)

    for copy in gather_coeff:
        copy.wait_recv()
    ck = cg[0, 0] + cg[0, 1]
    cshape = ck.shape
    row = iota(cshape, 1)
    plane = iota(cshape, 0)
    box_in = iota(cshape, 2) < 2 * qz
    nx, ny = 2 * qx, 2 * qy
    cw = faces(ck)
    half = 0.5 * ck
    cwx = jnp.where(plane < nx - 1, cw[0], 0.0)
    cwy = jnp.where(row < ny - 1, cw[1], 0.0)
    cw = (cwx, cwy, cw[2])
    cdiag = diagonal(cw)
    cdiag = cdiag + jnp.where(plane == 0, half, 0.0) + jnp.where(plane == nx - 1, half, 0.0)
    cdiag = cdiag + jnp.where(row == 0, half, 0.0) + jnp.where(row == ny - 1, half, 0.0)
    civ = jnp.where(box_in, 1.0 / cdiag, 0.0)

    finish_send(fine_round)
    finish_send(coeff_round)
    for copy in gather_coeff:
        copy.wait_send()

    def put_rhs(i, values):
        mf[i] = values
        if 1 <= i < mx - 1:
            va[i] = omega_first * values * miv[i]

    middle_finish(1, rhs_round, put_rhs)

    def middle_pre(i):
        vb[i] = plane_sweep(middle_w, mf[i], va, i, omega_second)

    def middle_leftover(i):
        va[i] = plane_left(middle_w, mf[i], vb, i)

    run(2, mx - 2, middle_pre)
    run(3, mx - 3, middle_leftover)

    pieces = []
    for i in range(qx):
        c = hx + 2 * i
        cs[i] = (va[c - 1] + va[c + 2]) * 0.5 + (va[c] + va[c + 1]) * 1.5
        pieces.append(restrict_rows(lambda first: cs[i, pl.ds(first, qy, stride=2), :]))
    rhs = times(jnp.concatenate(pieces, axis=0), to_coarse_z)
    for i in range(qx):
        cg[1, 0, px * qx + i, line, :] = rhs[i * qy : (i + 1) * qy]
    gather_rhs = gather_start(1)
    finish_send(rhs_round)
    for copy in gather_rhs:
        copy.wait_recv()

    cf = cg[1, 0] + cg[1, 1]
    c1 = omega_first * cf * civ
    c2 = sweep(cw, civ, c1, cf, omega_second)
    flat = c2.reshape(nx * ny, mz)
    correction = weigh(back_xy, times(flat, back_z))
    for i in range(hx):
        fixed = vb[hx + i, T : T + hy, :] + correction[i * hy : (i + 1) * hy]
        mid[2, hx + i, T : T + hy, :] = fixed
    last_round = middle_start(2)
    for copy in gather_rhs:
        copy.wait_send()

    def put_last(i, values):
        vc[i] = values

    middle_finish(2, last_round, put_last)

    def middle_post_first(i):
        va[i] = plane_sweep(middle_w, mf[i], vc, i, omega_first)

    def middle_post_second(i):
        vb[i] = plane_sweep(middle_w, mf[i], va, i, omega_second)

    run(1, mx - 1, middle_post_first)
    run(2, mx - 2, middle_post_second)

    low = hx - 2
    spread = times(vb[low : 2 * hx + 2].reshape((hx + 4) * my, mz), to_fine_z)
    for i in range(2, ex - 2):
        c = (i - H + 64) // 2 - 32 + hx - low
        other = c - 1 if i % 2 == 0 else c + 1
        mixed = 0.75 * spread[c * my : (c + 1) * my] + 0.25 * spread[other * my : (other + 1) * my]
        near = 0.75 * mixed
        even = near + 0.25 * shift(mixed, 0, -1)
        odd = near + 0.25 * shift(mixed, 0, 1)
        for t in range(2):
            lanes = slice(t * cz_, (t + 1) * cz_)
            fs[t, i - 2, pl.ds(0, my, stride=2), :] = even[:, lanes]
            fs[t, i - 2, pl.ds(1, my, stride=2), :] = odd[:, lanes]
    for i in range(2, ex - 2):
        rows = slice(2 * T - T, 2 * T - T + ey)
        fresh = jnp.concatenate([fs[0, i - 2, rows, :], fs[1, i - 2, rows, :]], axis=1)
        ua[i] = jnp.where(fine_in & plane_in(i), ub[i] + fresh, 0.0)

    def post(i):
        ub[i] = plane_sweep(fine_w, ks[1, i], ua, i, omega_first)

    def last(i):
        result = plane_sweep(fine_w, ks[1, i], ub, i, omega_second)
        out_ref[i - H] = result[T : T + cy, 0:cz_]

    run(3, ex - 3, post)
    run(H, H + cx, last)
    finish_send(last_round)


def solution(mesh):
    sizes = {axis: mesh.shape[axis] for axis in mesh.axis_names}
    spec = P("gx", "gy", "gz")

    def local(source, conductivity):
        cx, cy, cz = source.shape
        fine = (cx + 2 * H, cy + 2 * T, 2 * cz)
        mid = (cx // 2 * 3, cy // 2 + 2 * T, cz)
        vmem = pltpu.VMEM
        call = pl.pallas_call(
            functools.partial(kernel, sizes),
            out_shape=jax.ShapeDtypeStruct(source.shape, F32),
            in_specs=[pl.BlockSpec(memory_space=pltpu.HBM)] * 2,
            out_specs=pl.BlockSpec(memory_space=vmem),
            scratch_shapes=[
                vmem((2,) + fine, F32),
                vmem((cy, cz), F32),
                vmem((3, cy + 2 * T, cz), F32),
                vmem((3, cy + 2 * T, cz), F32),
                *[vmem(fine, F32)] * 8,
                vmem((2, cx // 2, cy + 2 * T, cz), F32),
                vmem((2, cx + 4, 2 * mid[1], cz), F32),
                vmem((cx // 4, mid[1], cz), F32),
                *[vmem(mid, F32)] * 10,
                vmem((3,) + mid, F32),
                vmem((3, cy // 2, cz), F32),
                vmem((3, 3) + mid[1:], F32),
                vmem((3, 3) + mid[1:], F32),
                vmem((2, 2, cx // 2, cy // 2, cz), F32),
                pltpu.SemaphoreType.DMA((copies,)),
                pltpu.SemaphoreType.DMA((copies,)),
                pltpu.SemaphoreType.DMA((2,)),
            ],
            compiler_params=pltpu.CompilerParams(
                collective_id=0, has_side_effects=True, vmem_limit_bytes=48 * 2**20
            ),
        )
        return call(*(pltpu.with_memory_space_constraint(v, pltpu.HBM) for v in (source, conductivity)))

    return jax.shard_map(
        local, mesh=mesh, in_specs=(spec, spec), out_specs=spec, check_vma=False
    )
```

```python
import functools
import math

import jax
import jax.numpy as jnp
from jax import lax
from jax.experimental import pallas as pl
from jax.experimental.pallas import tpu as pltpu
from jax.sharding import PartitionSpec as P

spectrum_top = 1.9
spectrum_low = 0.475
omega_first = 1.0 / (
    (spectrum_top + spectrum_low) / 2 + (spectrum_top - spectrum_low) / 2 * math.cos(math.pi / 4)
)
omega_second = 1.0 / (
    (spectrum_top + spectrum_low) / 2
    + (spectrum_top - spectrum_low) / 2 * math.cos(3 * math.pi / 4)
)
F32 = jnp.float32
MESH = pl.DeviceIdType.MESH
H = 4
T = 8


def iota(shape, dim):
    return lax.broadcasted_iota(jnp.int32, shape, dim)


def parts(values):
    high = values.astype(jnp.bfloat16)
    rest = values - high.astype(F32)
    middle = rest.astype(jnp.bfloat16)
    return [high, middle, (rest - middle.astype(F32)).astype(jnp.bfloat16)]


def times(values, weights):
    size = values.shape[0]
    result = jnp.dot(
        jnp.concatenate(parts(values), axis=0),
        weights.astype(jnp.bfloat16),
        preferred_element_type=F32,
    )
    return result[:size] + (result[size : 2 * size] + result[2 * size :])


def weigh(weights, values):
    return jnp.dot(
        jnp.concatenate([weights.astype(jnp.bfloat16)] * 3, axis=1),
        jnp.concatenate(parts(values), axis=0),
        preferred_element_type=F32,
    )


def ring(index, size, cut):
    return jnp.where(index >= cut, index - size, index)


def restrict_weight(diff):
    side = (diff == -1) | (diff == 2)
    centre = (diff == 0) | (diff == 1)
    return jnp.where(centre, 0.375, jnp.where(side, 0.125, 0.0)).astype(F32)


def mean_weight(diff):
    return jnp.where((diff == 0) | (diff == 1), 0.5, 0.0).astype(F32)


def interpolate_weight(fine, coarse):
    base = (fine + 64) // 2 - 32
    other = base + jnp.where((fine + 64) % 2 == 0, -1, 1)
    return jnp.where(coarse == base, 0.75, jnp.where(coarse == other, 0.25, 0.0)).astype(F32)


def shift(values, axis, amount):
    size = values.shape[axis]
    return pltpu.roll(values, (-amount) % size, axis)


def span(way, extent, halo):
    if way == 0:
        return pl.ds(halo, extent), pl.ds(halo, extent)
    if way > 0:
        return pl.ds(extent, halo), pl.ds(0, halo)
    return pl.ds(halo, halo), pl.ds(halo + extent, halo)


ways = (0, 1, -1)
others = [(a, b, c) for c in ways for b in ways for a in ways if (a, b, c) != (0, 0, 0)]
mates = [(a, b, c) for a in (0, 1) for b in (0, 1) for c in (0, 1) if (a, b, c) != (0, 0, 0)]
axes = ("gx", "gy", "gz")
copies = 4 * len(others) + 2 * len(mates)


def kernel(
    sizes, s_ref, k_ref, out_ref,
    ks, pk, qa, qb, wx, wy, wz, dg, iv, ua, ub, left, rs, fs, cs,
    mk, mf, mwx, mwy, mwz, mdg, miv, va, vb, vc,
    mid, mp, ma, mb, cg, send_sem, recv_sem, load_sem,
):
    cx, cy, cz_ = s_ref.shape
    hx, hy, hz = cx // 2, cy // 2, cz_ // 2
    qx, qy, qz = cx // 4, cy // 4, cz_ // 4
    ex, ey, ez = ks.shape[1:]
    mx, my, mz = mid.shape[1:]
    pos = {axis: lax.axis_index(axis) for axis in axes}
    used = [0]

    def has(offset, sign):
        here = None
        for axis, way in zip(axes, offset):
            if way != 0:
                good = pos[axis] < sizes[axis] - 1 if way * sign > 0 else pos[axis] > 0
                here = good if here is None else here & good
        return here

    def make(offset, src, dst, number):
        return pltpu.make_async_remote_copy(
            src_ref=src, dst_ref=dst, send_sem=send_sem.at[number], recv_sem=recv_sem.at[number],
            device_id={axis: pos[axis] + way for axis, way in zip(axes, offset)},
            device_id_type=MESH,
        )

    def start(items):
        started = []
        for offset, src, dst in items:
            number = used[0]
            used[0] += 1
            started.append((offset, src, dst, number))

            @pl.when(has(offset, 1))
            def _():
                make(offset, src, dst, number).start()

        return started

    def finish_recv(started, wanted=lambda offset: True):
        for offset, src, dst, number in started:
            if not wanted(offset):
                continue

            @pl.when(has(offset, -1))
            def _():
                make(offset, src, dst, number).wait_recv()

    def finish_send(started):
        for offset, src, dst, number in started:

            @pl.when(has(offset, 1))
            def _():
                make(offset, src, dst, number).wait_send()

    loads = []
    for f, ref in enumerate((k_ref, s_ref)):
        own = ks.at[f, pl.ds(H, cx), pl.ds(T, cy), pl.ds(0, cz_)]
        loads.append(pltpu.make_async_copy(ref, own, load_sem.at[f]))
        loads[f].start()
    for f in range(2):
        for i in range(ex):
            if H <= i < H + cx:
                ks[f, i, 0:T, 0:cz_] = jnp.zeros((T, cz_), F32)
                ks[f, i, T + cy : ey, 0:cz_] = jnp.zeros((T, cz_), F32)
            else:
                ks[f, i, :, 0:cz_] = jnp.zeros((ey, cz_), F32)
    qa[...] = jnp.zeros(qa.shape, F32)
    qb[...] = jnp.zeros(qb.shape, F32)
    mid[...] = jnp.zeros(mid.shape, F32)
    ma[...] = jnp.zeros(ma.shape, F32)
    mb[...] = jnp.zeros(mb.shape, F32)
    barrier = pltpu.get_barrier_semaphore()
    count = 0
    for offset in others:
        here = has(offset, 1)
        count = count + here.astype(jnp.int32)

        @pl.when(here)
        def _():
            pl.semaphore_signal(
                barrier, inc=1,
                device_id={axis: pos[axis] + way for axis, way in zip(axes, offset)},
                device_id_type=MESH,
            )

    group = iota((cy, cz_), 1) // (2 * H)
    packed = jnp.zeros((cy, cz_), F32)
    for f in range(2):
        loads[f].wait()
        for p in range(cx):
            g = f * cx + p
            own = ks[f, H + p, T : T + cy, 0:cz_]
            packed = jnp.where(group == g, shift(own, 1, -(H + 2 * H * g)), packed)
    pk[...] = packed
    pl.semaphore_wait(barrier, count)

    main = pl.ds(0, cz_)
    items = []
    for offset in others:
        dx, dy, dz = offset
        xs, xd = span(dx, cx, H)
        ys, yd = span(dy, cy, T)
        if dz == 0:
            items.append((offset, ks.at[:, xs, ys, main], ks.at[:, xd, yd, main]))
        else:
            target = qa if dz > 0 else qb
            rows = pl.ds(ys.start - T, ys.size)
            items.append((offset, pk.at[rows], target.at[1 - dx, yd]))
    fine_round = start(items)

    mgroup = iota((hy, mz), 1) // H

    def middle_start(f):
        packed = jnp.zeros((hy, mz), F32)
        for p in range(hx):
            own = mid[f, hx + p, T : T + hy, :]
            packed = jnp.where(mgroup == 2 * p, shift(own, 1, hz - H - 2 * H * p), packed)
            packed = jnp.where(mgroup == 2 * p + 1, shift(own, 1, -(2 * H * p + H)), packed)
        mp[f] = packed
        items = []
        for offset in others:
            dx, dy, dz = offset
            xs, xd = span(dx, hx, hx)
            ys, yd = span(dy, hy, T)
            if dz == 0:
                items.append((offset, mid.at[f, xs, ys], mid.at[f, xd, yd]))
            else:
                target = ma if dz > 0 else mb
                rows = pl.ds(ys.start - T, ys.size)
                items.append((offset, mp.at[f, rows], target.at[f, 1 - dx, yd]))
        return start(items)

    mlane = iota((my, mz), 1)

    def middle_finish(f, started, put):
        finish_recv(started)
        for i in range(mx):
            block, p = i // hx, i % hx
            right = shift(mb[f, block], 1, 2 * H * p + H - hz)
            left_side = shift(ma[f, block], 1, 2 * H * p - (mz - H))
            side = jnp.where(mlane < (hz + mz) // 2, right, left_side)
            put(i, jnp.where(mlane < hz, mid[f, i], side))

    px, py, pz = (pos[axis] % 2 for axis in axes)
    here = pl.ds(px * qx, qx)
    line = pl.ds(pl.multiple_of(py * qy, qy), qy)

    def gather_make(f, flips, number):
        return pltpu.make_async_remote_copy(
            src_ref=cg.at[f, 0, here, line], dst_ref=cg.at[f, flips[2], here, line],
            send_sem=send_sem.at[number], recv_sem=recv_sem.at[number],
            device_id={
                axis: pos[axis] + (1 - 2 * (pos[axis] % 2)) * flip for axis, flip in zip(axes, flips)
            },
            device_id_type=MESH,
        )

    def gather_start(f):
        started = []
        for flips in mates:
            copy = gather_make(f, flips, used[0])
            used[0] += 1
            copy.start()
            started.append(copy)
        return started

    lz = iota((cz_, mz), 0) - 2 * iota((cz_, mz), 1)
    mean_z = jnp.where(iota((cz_, mz), 1) < hz, mean_weight(lz), 0.0)
    for i in range(hx):
        own = [ks[0, H + 2 * i + j, T : T + cy, 0:cz_] for j in range(2)]
        rs[0, i, T : T + cy, :] = (own[0] + own[1]) * 0.5
    means = [
        (rs[0, i, pl.ds(T, hy, stride=2), :] + rs[0, i, pl.ds(T + 1, hy, stride=2), :]) * 0.5
        for i in range(hx)
    ]
    means = times(jnp.concatenate(means, axis=0), mean_z)
    for i in range(hx):
        mid[0, hx + i, T : T + hy, :] = means[i * hy : (i + 1) * hy]
    coeff_round = middle_start(0)

    cj = iota((mz, mz), 1) - pz * qz
    clz = ring(iota((mz, mz), 0), mz, (hz + mz) // 2) - 2 * cj
    ckeep = (cj >= 0) & (cj < qz)
    to_coarse_z = jnp.where(ckeep, restrict_weight(clz), 0.0)
    cmean_z = jnp.where(ckeep, mean_weight(clz), 0.0)
    for i in range(qx):
        own_rows = [mid[0, hx + 2 * i + j, T : T + hy, :] for j in range(2)]
        cs[i, T : T + hy, :] = (own_rows[0] + own_rows[1]) * 0.5
    means = [
        (cs[i, pl.ds(T, qy, stride=2), :] + cs[i, pl.ds(T + 1, qy, stride=2), :]) * 0.5
        for i in range(qx)
    ]
    means = times(jnp.concatenate(means, axis=0), cmean_z)
    for i in range(qx):
        cg[0, 0, px * qx + i, line, :] = means[i * qy : (i + 1) * qy]
    gather_coeff = gather_start(0)

    r = iota((ey, ez), 0) - T + pos["gy"] * cy
    local_z = ring(iota((ey, ez), 1), ez, ez - cz_ // 2)
    z = local_z + pos["gz"] * cz_
    fine_in = (r >= 0) & (r < cy * sizes["gy"]) & (z >= 0) & (z < cz_ * sizes["gz"])
    fine_in = fine_in & (local_z >= -H) & (local_z < cz_ + H)

    def plane_in(i):
        x = i - H + pos["gx"] * cx
        return (x >= 0) & (x < cx * sizes["gx"])

    lz = ring(iota((ez, mz), 0), ez, ez - cz_ // 2) - 2 * iota((ez, mz), 1)
    to_middle_z = jnp.where(iota((ez, mz), 1) < hz, restrict_weight(lz), 0.0)

    mr = iota((my, mz), 0) - T + pos["gy"] * hy
    mlz = ring(iota((my, mz), 1), mz, (hz + mz) // 2)
    mzz = mlz + pos["gz"] * hz
    middle_in = (
        (mr >= 0) & (mr < hy * sizes["gy"]) & (mzz >= 0) & (mzz < hz * sizes["gz"])
        & (mlz >= -H) & (mlz < hz + H)
    )

    def middle_plane_in(i):
        x = i - hx + pos["gx"] * hx
        return (x >= 0) & (x < hx * sizes["gx"])

    jj = iota((mz, mz), 1)
    back_z = interpolate_weight(jj + pz * hz, iota((mz, mz), 0))
    back_z = jnp.where((jj < hz) & (iota((mz, mz), 0) < 2 * qz), back_z, 0.0)
    shape = (hx * hy, 4 * qx * qy)
    fine_i, coarse_i = iota(shape, 0), iota(shape, 1)
    back_xy = interpolate_weight(fine_i // hy + px * hx, coarse_i // (2 * qy)) * interpolate_weight(
        fine_i % hy + py * hy, coarse_i % (2 * qy)
    )
    fine_lane = ring(iota((mz, ez), 1), ez, ez - cz_ // 2)
    middle_lane = ring(iota((mz, ez), 0), mz, (hz + mz) // 2)
    wide = (fine_lane >= -H) & (fine_lane < cz_ + H)
    to_fine_z = jnp.where(wide, interpolate_weight(fine_lane, middle_lane), 0.0)

    lane = iota((ey, cz_), 1)

    def unpack(block):
        merged = jnp.where(lane % (2 * H) < H, qa[block], qb[block])
        for i in range(ex):
            if (i - H) // cx + 1 == block:
                for f in range(2):
                    p = (i - H) % cx
                    ks[f, i, :, cz_:ez] = shift(merged, 1, H + 2 * H * (f * cx + p))

    fine_w = (wx, wy, wz, dg, iv)
    middle_w = (mwx, mwy, mwz, mdg, miv)

    def set_weights(w, k_of, i, inside):
        ax, ay, az, diag_ref, inverse_ref = w
        k = k_of(i)
        after = 0.5 * (k + k_of(i + 1))
        a = 0.5 * (k + shift(k, 0, 1))
        b = 0.5 * (k + shift(k, 1, 1))
        diag = (ax[i - 1] + after) + (a + shift(a, 0, -1)) + (b + shift(b, 1, -1))
        ax[i] = after
        ay[i] = a
        az[i] = b
        diag_ref[i] = diag
        inverse = jnp.where(inside, 1.0 / diag, 0.0)
        inverse_ref[i] = inverse
        return inverse

    def around(w, u, i):
        v = u[i]
        a, b = w[1][i], w[2][i]
        total = w[0][i] * u[i + 1] + w[0][i - 1] * u[i - 1]
        total = total + (a * shift(v, 0, 1) + shift(a * v, 0, -1))
        total = total + (b * shift(v, 1, 1) + shift(b * v, 1, -1))
        return v, total

    def plane_sweep(w, f, u, i, omega):
        v, total = around(w, u, i)
        return (1.0 - omega) * v + omega * (f + total) * w[4][i]

    def plane_left(w, f, u, i):
        v, total = around(w, u, i)
        return jnp.where(w[4][i] > 0.0, f - w[3][i] * v + total, 0.0)

    def run(low, high, body):
        for i in range(low, high):
            body(i)

    def weights(i):
        inverse = set_weights(fine_w, lambda j: ks[0, j], i, fine_in & plane_in(i))
        ua[i] = omega_first * ks[1, i] * inverse

    def pre(i):
        ub[i] = plane_sweep(fine_w, ks[1, i], ua, i, omega_second)

    def leftover(i):
        left[i] = plane_left(fine_w, ks[1, i], ub, i)

    last_own = H + cx - 1
    finish_recv(fine_round, lambda offset: offset[0] == 0)
    unpack(1)
    wx[H] = 0.5 * (ks[0, H] + ks[0, H + 1])
    run(H + 1, last_own, weights)
    run(H + 2, last_own - 1, pre)
    run(H + 3, last_own - 2, leftover)
    finish_recv(fine_round, lambda offset: offset[0] != 0)
    unpack(0)
    unpack(2)
    wx[0] = 0.5 * (ks[0, 0] + ks[0, 1])
    run(1, H + 1, weights)
    run(last_own, ex - 1, weights)
    run(2, H + 2, pre)
    run(last_own - 1, ex - 2, pre)
    run(3, H + 3, leftover)
    run(last_own - 2, ex - 3, leftover)

    def restrict_rows(take):
        side = take(T - 1) + take(T + 2)
        return side * 0.125 + (take(T) + take(T + 1)) * 0.375

    pieces = []
    for i in range(hx):
        c = H + 2 * i
        mixed = (left[c - 1] + left[c + 2]) * 0.5 + (left[c] + left[c + 1]) * 1.5
        rs[0, i] = mixed[:, :cz_]
        rs[1, i] = mixed[:, cz_:]
        halves = [
            restrict_rows(lambda first: rs[t, i, pl.ds(first, hy, stride=2), :]) for t in range(2)
        ]
        pieces.append(jnp.concatenate(halves, axis=1))
    rhs = times(jnp.concatenate(pieces, axis=0), to_middle_z)
    for i in range(hx):
        mid[1, hx + i, T : T + hy, :] = rhs[i * hy : (i + 1) * hy]
    rhs_round = middle_start(1)

    def up(values):
        return jnp.concatenate([values[1:], values[:1]], axis=0)

    def down(values):
        return jnp.concatenate([values[-1:], values[:-1]], axis=0)

    def faces(k):
        return 0.5 * (k + up(k)), 0.5 * (k + shift(k, 1, 1)), 0.5 * (k + shift(k, 2, 1))

    def diagonal(w):
        return (w[0] + down(w[0])) + (w[1] + shift(w[1], 1, -1)) + (w[2] + shift(w[2], 2, -1))

    def neighbours(w, v):
        total = w[0] * up(v) + down(w[0] * v)
        total = total + (w[1] * shift(v, 1, 1) + shift(w[1] * v, 1, -1))
        return total + (w[2] * shift(v, 2, 1) + shift(w[2] * v, 2, -1))

    def sweep(w, inverse, v, f, omega):
        return (1.0 - omega) * v + omega * (f + neighbours(w, v)) * inverse

    def put_coeff(i, values):
        mk[i] = values

    middle_finish(0, coeff_round, put_coeff)
    mwx[0] = 0.5 * (mk[0] + mk[1])

    def middle_weights(i):
        set_weights(middle_w, lambda j: mk[j], i, middle_in & middle_plane_in(i))

    run(1, mx - 1, middle_weights)

    for copy in gather_coeff:
        copy.wait_recv()
    ck = cg[0, 0] + cg[0, 1]
    cshape = ck.shape
    row = iota(cshape, 1)
    plane = iota(cshape, 0)
    box_in = iota(cshape, 2) < 2 * qz
    nx, ny = 2 * qx, 2 * qy
    cw = faces(ck)
    half = 0.5 * ck
    cwx = jnp.where(plane < nx - 1, cw[0], 0.0)
    cwy = jnp.where(row < ny - 1, cw[1], 0.0)
    cw = (cwx, cwy, cw[2])
    cdiag = diagonal(cw)
    cdiag = cdiag + jnp.where(plane == 0, half, 0.0) + jnp.where(plane == nx - 1, half, 0.0)
    cdiag = cdiag + jnp.where(row == 0, half, 0.0) + jnp.where(row == ny - 1, half, 0.0)
    civ = jnp.where(box_in, 1.0 / cdiag, 0.0)

    finish_send(fine_round)
    finish_send(coeff_round)
    for copy in gather_coeff:
        copy.wait_send()

    def put_rhs(i, values):
        mf[i] = values
        if 1 <= i < mx - 1:
            va[i] = omega_first * values * miv[i]

    middle_finish(1, rhs_round, put_rhs)

    def middle_pre(i):
        vb[i] = plane_sweep(middle_w, mf[i], va, i, omega_second)

    def middle_leftover(i):
        va[i] = plane_left(middle_w, mf[i], vb, i)

    run(2, mx - 2, middle_pre)
    run(3, mx - 3, middle_leftover)

    pieces = []
    for i in range(qx):
        c = hx + 2 * i
        cs[i] = (va[c - 1] + va[c + 2]) * 0.5 + (va[c] + va[c + 1]) * 1.5
        pieces.append(restrict_rows(lambda first: cs[i, pl.ds(first, qy, stride=2), :]))
    rhs = times(jnp.concatenate(pieces, axis=0), to_coarse_z)
    for i in range(qx):
        cg[1, 0, px * qx + i, line, :] = rhs[i * qy : (i + 1) * qy]
    gather_rhs = gather_start(1)
    finish_send(rhs_round)
    for copy in gather_rhs:
        copy.wait_recv()

    cf = cg[1, 0] + cg[1, 1]
    c1 = omega_first * cf * civ
    c2 = sweep(cw, civ, c1, cf, omega_second)
    flat = c2.reshape(nx * ny, mz)
    correction = weigh(back_xy, times(flat, back_z))
    for i in range(hx):
        fixed = vb[hx + i, T : T + hy, :] + correction[i * hy : (i + 1) * hy]
        mid[2, hx + i, T : T + hy, :] = fixed
    last_round = middle_start(2)
    for copy in gather_rhs:
        copy.wait_send()

    def put_last(i, values):
        vc[i] = values

    middle_finish(2, last_round, put_last)

    def middle_post_first(i):
        va[i] = plane_sweep(middle_w, mf[i], vc, i, omega_first)

    def middle_post_second(i):
        vb[i] = plane_sweep(middle_w, mf[i], va, i, omega_second)

    run(1, mx - 1, middle_post_first)
    run(2, mx - 2, middle_post_second)

    low = hx - 2
    spread = times(vb[low : 2 * hx + 2].reshape((hx + 4) * my, mz), to_fine_z)
    for i in range(2, ex - 2):
        c = (i - H + 64) // 2 - 32 + hx - low
        other = c - 1 if i % 2 == 0 else c + 1
        mixed = 0.75 * spread[c * my : (c + 1) * my] + 0.25 * spread[other * my : (other + 1) * my]
        near = 0.75 * mixed
        even = near + 0.25 * shift(mixed, 0, -1)
        odd = near + 0.25 * shift(mixed, 0, 1)
        for t in range(2):
            lanes = slice(t * cz_, (t + 1) * cz_)
            fs[t, i - 2, pl.ds(0, my, stride=2), :] = even[:, lanes]
            fs[t, i - 2, pl.ds(1, my, stride=2), :] = odd[:, lanes]
    for i in range(2, ex - 2):
        rows = slice(2 * T - T, 2 * T - T + ey)
        fresh = jnp.concatenate([fs[0, i - 2, rows, :], fs[1, i - 2, rows, :]], axis=1)
        ua[i] = jnp.where(fine_in & plane_in(i), ub[i] + fresh, 0.0)

    def post(i):
        ub[i] = plane_sweep(fine_w, ks[1, i], ua, i, omega_first)

    def last(i):
        result = plane_sweep(fine_w, ks[1, i], ub, i, omega_second)
        out_ref[i - H] = result[T : T + cy, 0:cz_]

    run(3, ex - 3, post)
    run(H, H + cx, last)
    finish_send(last_round)


def solution(mesh):
    sizes = {axis: mesh.shape[axis] for axis in mesh.axis_names}
    spec = P("gx", "gy", "gz")

    def local(source, conductivity):
        cx, cy, cz = source.shape
        fine = (cx + 2 * H, cy + 2 * T, 2 * cz)
        mid = (cx // 2 * 3, cy // 2 + 2 * T, cz)
        vmem = pltpu.VMEM
        call = pl.pallas_call(
            functools.partial(kernel, sizes),
            out_shape=jax.ShapeDtypeStruct(source.shape, F32),
            in_specs=[pl.BlockSpec(memory_space=pltpu.HBM)] * 2,
            out_specs=pl.BlockSpec(memory_space=vmem),
            scratch_shapes=[
                vmem((2,) + fine, F32),
                vmem((cy, cz), F32),
                vmem((3, cy + 2 * T, cz), F32),
                vmem((3, cy + 2 * T, cz), F32),
                *[vmem(fine, F32)] * 8,
                vmem((2, cx // 2, cy + 2 * T, cz), F32),
                vmem((2, cx + 4, 2 * mid[1], cz), F32),
                vmem((cx // 4, mid[1], cz), F32),
                *[vmem(mid, F32)] * 10,
                vmem((3,) + mid, F32),
                vmem((3, cy // 2, cz), F32),
                vmem((3, 3) + mid[1:], F32),
                vmem((3, 3) + mid[1:], F32),
                vmem((2, 2, cx // 2, cy // 2, cz), F32),
                pltpu.SemaphoreType.DMA((copies,)),
                pltpu.SemaphoreType.DMA((copies,)),
                pltpu.SemaphoreType.DMA((2,)),
            ],
            compiler_params=pltpu.CompilerParams(
                collective_id=0, has_side_effects=True, vmem_limit_bytes=48 * 2**20
            ),
        )
        return call(*(pltpu.with_memory_space_constraint(v, pltpu.HBM) for v in (source, conductivity)))

    return jax.shard_map(
        local, mesh=mesh, in_specs=(spec, spec), out_specs=spec, check_vma=False
    )
```

```python
import functools
import math

import jax
import jax.numpy as jnp
from jax import lax
from jax.experimental import pallas as pl
from jax.experimental.pallas import tpu as pltpu
from jax.sharding import PartitionSpec as P

spectrum_top = 1.9
spectrum_low = 0.475
omega_first = 1.0 / (
    (spectrum_top + spectrum_low) / 2 + (spectrum_top - spectrum_low) / 2 * math.cos(math.pi / 4)
)
omega_second = 1.0 / (
    (spectrum_top + spectrum_low) / 2
    + (spectrum_top - spectrum_low) / 2 * math.cos(3 * math.pi / 4)
)
F32 = jnp.float32
MESH = pl.DeviceIdType.MESH
H = 4
T = 8


def iota(shape, dim):
    return lax.broadcasted_iota(jnp.int32, shape, dim)


def parts(values):
    high = values.astype(jnp.bfloat16)
    rest = values - high.astype(F32)
    middle = rest.astype(jnp.bfloat16)
    return [high, middle, (rest - middle.astype(F32)).astype(jnp.bfloat16)]


def times(values, weights):
    size = values.shape[0]
    result = jnp.dot(
        jnp.concatenate(parts(values), axis=0),
        weights.astype(jnp.bfloat16),
        preferred_element_type=F32,
    )
    return result[:size] + (result[size : 2 * size] + result[2 * size :])


def weigh(weights, values):
    return jnp.dot(
        jnp.concatenate([weights.astype(jnp.bfloat16)] * 3, axis=1),
        jnp.concatenate(parts(values), axis=0),
        preferred_element_type=F32,
    )


def ring(index, size, cut):
    return jnp.where(index >= cut, index - size, index)


def restrict_weight(diff):
    side = (diff == -1) | (diff == 2)
    centre = (diff == 0) | (diff == 1)
    return jnp.where(centre, 0.375, jnp.where(side, 0.125, 0.0)).astype(F32)


def mean_weight(diff):
    return jnp.where((diff == 0) | (diff == 1), 0.5, 0.0).astype(F32)


def interpolate_weight(fine, coarse):
    base = (fine + 64) // 2 - 32
    other = base + jnp.where((fine + 64) % 2 == 0, -1, 1)
    return jnp.where(coarse == base, 0.75, jnp.where(coarse == other, 0.25, 0.0)).astype(F32)


def shift(values, axis, amount):
    size = values.shape[axis]
    return pltpu.roll(values, (-amount) % size, axis)


def span(way, extent, halo):
    if way == 0:
        return pl.ds(halo, extent), pl.ds(halo, extent)
    if way > 0:
        return pl.ds(extent, halo), pl.ds(0, halo)
    return pl.ds(halo, halo), pl.ds(halo + extent, halo)


ways = (0, 1, -1)
others = [(a, b, c) for c in ways for b in ways for a in ways if (a, b, c) != (0, 0, 0)]
mates = [(a, b, c) for a in (0, 1) for b in (0, 1) for c in (0, 1) if (a, b, c) != (0, 0, 0)]
axes = ("gx", "gy", "gz")
copies = 4 * len(others) + 2 * len(mates)


def kernel(
    sizes, s_ref, k_ref, out_ref,
    ks, pk, qa, qb, wx, wy, wz, dg, iv, ua, ub, left, rs, fs, cs,
    mk, mf, mwx, mwy, mwz, mdg, miv, va, vb, vc,
    mid, mp, ma, mb, cg, send_sem, recv_sem, load_sem,
):
    cx, cy, cz_ = s_ref.shape
    hx, hy, hz = cx // 2, cy // 2, cz_ // 2
    qx, qy, qz = cx // 4, cy // 4, cz_ // 4
    ex, ey, ez = ks.shape[1:]
    mx, my, mz = mid.shape[1:]
    pos = {axis: lax.axis_index(axis) for axis in axes}
    used = [0]

    def has(offset, sign):
        here = None
        for axis, way in zip(axes, offset):
            if way != 0:
                good = pos[axis] < sizes[axis] - 1 if way * sign > 0 else pos[axis] > 0
                here = good if here is None else here & good
        return here

    def make(offset, src, dst, number):
        return pltpu.make_async_remote_copy(
            src_ref=src, dst_ref=dst, send_sem=send_sem.at[number], recv_sem=recv_sem.at[number],
            device_id={axis: pos[axis] + way for axis, way in zip(axes, offset)},
            device_id_type=MESH,
        )

    def start(items):
        started = []
        for offset, src, dst in items:
            number = used[0]
            used[0] += 1
            started.append((offset, src, dst, number))

            @pl.when(has(offset, 1))
            def _():
                make(offset, src, dst, number).start()

        return started

    def finish_recv(started, wanted=lambda offset: True):
        for offset, src, dst, number in started:
            if not wanted(offset):
                continue

            @pl.when(has(offset, -1))
            def _():
                make(offset, src, dst, number).wait_recv()

    def finish_send(started):
        for offset, src, dst, number in started:

            @pl.when(has(offset, 1))
            def _():
                make(offset, src, dst, number).wait_send()

    loads = []
    for f, ref in enumerate((k_ref, s_ref)):
        own = ks.at[f, pl.ds(H, cx), pl.ds(T, cy), pl.ds(0, cz_)]
        loads.append(pltpu.make_async_copy(ref, own, load_sem.at[f]))
        loads[f].start()
    for f in range(2):
        for i in range(ex):
            if H <= i < H + cx:
                ks[f, i, 0:T, 0:cz_] = jnp.zeros((T, cz_), F32)
                ks[f, i, T + cy : ey, 0:cz_] = jnp.zeros((T, cz_), F32)
            else:
                ks[f, i, :, 0:cz_] = jnp.zeros((ey, cz_), F32)
    qa[...] = jnp.zeros(qa.shape, F32)
    qb[...] = jnp.zeros(qb.shape, F32)
    mid[...] = jnp.zeros(mid.shape, F32)
    ma[...] = jnp.zeros(ma.shape, F32)
    mb[...] = jnp.zeros(mb.shape, F32)
    barrier = pltpu.get_barrier_semaphore()
    count = 0
    for offset in others:
        here = has(offset, 1)
        count = count + here.astype(jnp.int32)

        @pl.when(here)
        def _():
            pl.semaphore_signal(
                barrier, inc=1,
                device_id={axis: pos[axis] + way for axis, way in zip(axes, offset)},
                device_id_type=MESH,
            )

    group = iota((cy, cz_), 1) // (2 * H)
    packed = jnp.zeros((cy, cz_), F32)
    for f in range(2):
        loads[f].wait()
        for p in range(cx):
            g = f * cx + p
            own = ks[f, H + p, T : T + cy, 0:cz_]
            packed = jnp.where(group == g, shift(own, 1, -(H + 2 * H * g)), packed)
    pk[...] = packed
    pl.semaphore_wait(barrier, count)

    main = pl.ds(0, cz_)
    items = []
    for offset in others:
        dx, dy, dz = offset
        xs, xd = span(dx, cx, H)
        ys, yd = span(dy, cy, T)
        if dz == 0:
            items.append((offset, ks.at[:, xs, ys, main], ks.at[:, xd, yd, main]))
        else:
            target = qa if dz > 0 else qb
            rows = pl.ds(ys.start - T, ys.size)
            items.append((offset, pk.at[rows], target.at[1 - dx, yd]))
    fine_round = start(items)

    mgroup = iota((hy, mz), 1) // H

    def middle_start(f):
        packed = jnp.zeros((hy, mz), F32)
        for p in range(hx):
            own = mid[f, hx + p, T : T + hy, :]
            packed = jnp.where(mgroup == 2 * p, shift(own, 1, hz - H - 2 * H * p), packed)
            packed = jnp.where(mgroup == 2 * p + 1, shift(own, 1, -(2 * H * p + H)), packed)
        mp[f] = packed
        items = []
        for offset in others:
            dx, dy, dz = offset
            xs, xd = span(dx, hx, hx)
            ys, yd = span(dy, hy, T)
            if dz == 0:
                items.append((offset, mid.at[f, xs, ys], mid.at[f, xd, yd]))
            else:
                target = ma if dz > 0 else mb
                rows = pl.ds(ys.start - T, ys.size)
                items.append((offset, mp.at[f, rows], target.at[f, 1 - dx, yd]))
        return start(items)

    mlane = iota((my, mz), 1)

    def middle_finish(f, started, put):
        finish_recv(started)
        for i in range(mx):
            block, p = i // hx, i % hx
            right = shift(mb[f, block], 1, 2 * H * p + H - hz)
            left_side = shift(ma[f, block], 1, 2 * H * p - (mz - H))
            side = jnp.where(mlane < (hz + mz) // 2, right, left_side)
            put(i, jnp.where(mlane < hz, mid[f, i], side))

    px, py, pz = (pos[axis] % 2 for axis in axes)
    here = pl.ds(px * qx, qx)
    line = pl.ds(pl.multiple_of(py * qy, qy), qy)

    def gather_make(f, flips, number):
        return pltpu.make_async_remote_copy(
            src_ref=cg.at[f, 0, here, line], dst_ref=cg.at[f, flips[2], here, line],
            send_sem=send_sem.at[number], recv_sem=recv_sem.at[number],
            device_id={
                axis: pos[axis] + (1 - 2 * (pos[axis] % 2)) * flip for axis, flip in zip(axes, flips)
            },
            device_id_type=MESH,
        )

    def gather_start(f):
        started = []
        for flips in mates:
            copy = gather_make(f, flips, used[0])
            used[0] += 1
            copy.start()
            started.append(copy)
        return started

    lz = iota((cz_, mz), 0) - 2 * iota((cz_, mz), 1)
    mean_z = jnp.where(iota((cz_, mz), 1) < hz, mean_weight(lz), 0.0)
    for i in range(hx):
        own = [ks[0, H + 2 * i + j, T : T + cy, 0:cz_] for j in range(2)]
        rs[0, i, T : T + cy, :] = (own[0] + own[1]) * 0.5
    means = [
        (rs[0, i, pl.ds(T, hy, stride=2), :] + rs[0, i, pl.ds(T + 1, hy, stride=2), :]) * 0.5
        for i in range(hx)
    ]
    means = times(jnp.concatenate(means, axis=0), mean_z)
    for i in range(hx):
        mid[0, hx + i, T : T + hy, :] = means[i * hy : (i + 1) * hy]
    coeff_round = middle_start(0)

    cj = iota((mz, mz), 1) - pz * qz
    clz = ring(iota((mz, mz), 0), mz, (hz + mz) // 2) - 2 * cj
    ckeep = (cj >= 0) & (cj < qz)
    to_coarse_z = jnp.where(ckeep, restrict_weight(clz), 0.0)
    cmean_z = jnp.where(ckeep, mean_weight(clz), 0.0)
    for i in range(qx):
        own_rows = [mid[0, hx + 2 * i + j, T : T + hy, :] for j in range(2)]
        cs[i, T : T + hy, :] = (own_rows[0] + own_rows[1]) * 0.5
    means = [
        (cs[i, pl.ds(T, qy, stride=2), :] + cs[i, pl.ds(T + 1, qy, stride=2), :]) * 0.5
        for i in range(qx)
    ]
    means = times(jnp.concatenate(means, axis=0), cmean_z)
    for i in range(qx):
        cg[0, 0, px * qx + i, line, :] = means[i * qy : (i + 1) * qy]
    gather_coeff = gather_start(0)

    r = iota((ey, ez), 0) - T + pos["gy"] * cy
    local_z = ring(iota((ey, ez), 1), ez, ez - cz_ // 2)
    z = local_z + pos["gz"] * cz_
    fine_in = (r >= 0) & (r < cy * sizes["gy"]) & (z >= 0) & (z < cz_ * sizes["gz"])
    fine_in = fine_in & (local_z >= -H) & (local_z < cz_ + H)

    def plane_in(i):
        x = i - H + pos["gx"] * cx
        return (x >= 0) & (x < cx * sizes["gx"])

    lz = ring(iota((ez, mz), 0), ez, ez - cz_ // 2) - 2 * iota((ez, mz), 1)
    to_middle_z = jnp.where(iota((ez, mz), 1) < hz, restrict_weight(lz), 0.0)

    mr = iota((my, mz), 0) - T + pos["gy"] * hy
    mlz = ring(iota((my, mz), 1), mz, (hz + mz) // 2)
    mzz = mlz + pos["gz"] * hz
    middle_in = (
        (mr >= 0) & (mr < hy * sizes["gy"]) & (mzz >= 0) & (mzz < hz * sizes["gz"])
        & (mlz >= -H) & (mlz < hz + H)
    )

    def middle_plane_in(i):
        x = i - hx + pos["gx"] * hx
        return (x >= 0) & (x < hx * sizes["gx"])

    jj = iota((mz, mz), 1)
    back_z = interpolate_weight(jj + pz * hz, iota((mz, mz), 0))
    back_z = jnp.where((jj < hz) & (iota((mz, mz), 0) < 2 * qz), back_z, 0.0)
    shape = (hx * hy, 4 * qx * qy)
    fine_i, coarse_i = iota(shape, 0), iota(shape, 1)
    back_xy = interpolate_weight(fine_i // hy + px * hx, coarse_i // (2 * qy)) * interpolate_weight(
        fine_i % hy + py * hy, coarse_i % (2 * qy)
    )
    fine_lane = ring(iota((mz, ez), 1), ez, ez - cz_ // 2)
    middle_lane = ring(iota((mz, ez), 0), mz, (hz + mz) // 2)
    wide = (fine_lane >= -H) & (fine_lane < cz_ + H)
    to_fine_z = jnp.where(wide, interpolate_weight(fine_lane, middle_lane), 0.0)

    lane = iota((ey, cz_), 1)

    def unpack(block):
        merged = jnp.where(lane % (2 * H) < H, qa[block], qb[block])
        for i in range(ex):
            if (i - H) // cx + 1 == block:
                for f in range(2):
                    p = (i - H) % cx
                    ks[f, i, :, cz_:ez] = shift(merged, 1, H + 2 * H * (f * cx + p))

    fine_w = (wx, wy, wz, dg, iv)
    middle_w = (mwx, mwy, mwz, mdg, miv)

    def set_weights(w, k_of, i, inside):
        ax, ay, az, diag_ref, inverse_ref = w
        k = k_of(i)
        after = 0.5 * (k + k_of(i + 1))
        a = 0.5 * (k + shift(k, 0, 1))
        b = 0.5 * (k + shift(k, 1, 1))
        diag = (ax[i - 1] + after) + (a + shift(a, 0, -1)) + (b + shift(b, 1, -1))
        ax[i] = after
        ay[i] = a
        az[i] = b
        diag_ref[i] = diag
        inverse = jnp.where(inside, 1.0 / diag, 0.0)
        inverse_ref[i] = inverse
        return inverse

    def around(w, u, i):
        v = u[i]
        a, b = w[1][i], w[2][i]
        total = w[0][i] * u[i + 1] + w[0][i - 1] * u[i - 1]
        total = total + (a * shift(v, 0, 1) + shift(a * v, 0, -1))
        total = total + (b * shift(v, 1, 1) + shift(b * v, 1, -1))
        return v, total

    def plane_sweep(w, f, u, i, omega):
        v, total = around(w, u, i)
        return (1.0 - omega) * v + omega * (f + total) * w[4][i]

    def plane_left(w, f, u, i):
        v, total = around(w, u, i)
        return jnp.where(w[4][i] > 0.0, f - w[3][i] * v + total, 0.0)

    def run(low, high, body):
        for i in range(low, high):
            body(i)

    def weights(i):
        inverse = set_weights(fine_w, lambda j: ks[0, j], i, fine_in & plane_in(i))
        ua[i] = omega_first * ks[1, i] * inverse

    def pre(i):
        ub[i] = plane_sweep(fine_w, ks[1, i], ua, i, omega_second)

    def leftover(i):
        left[i] = plane_left(fine_w, ks[1, i], ub, i)

    last_own = H + cx - 1
    finish_recv(fine_round, lambda offset: offset[0] == 0)
    unpack(1)
    wx[H] = 0.5 * (ks[0, H] + ks[0, H + 1])
    run(H + 1, last_own, weights)
    run(H + 2, last_own - 1, pre)
    run(H + 3, last_own - 2, leftover)
    finish_recv(fine_round, lambda offset: offset[0] != 0)
    unpack(0)
    unpack(2)
    wx[0] = 0.5 * (ks[0, 0] + ks[0, 1])
    run(1, H + 1, weights)
    run(last_own, ex - 1, weights)
    run(2, H + 2, pre)
    run(last_own - 1, ex - 2, pre)
    run(3, H + 3, leftover)
    run(last_own - 2, ex - 3, leftover)

    def restrict_rows(take):
        side = take(T - 1) + take(T + 2)
        return side * 0.125 + (take(T) + take(T + 1)) * 0.375

    pieces = []
    for i in range(hx):
        c = H + 2 * i
        mixed = (left[c - 1] + left[c + 2]) * 0.5 + (left[c] + left[c + 1]) * 1.5
        rs[0, i] = mixed[:, :cz_]
        rs[1, i] = mixed[:, cz_:]
        halves = [
            restrict_rows(lambda first: rs[t, i, pl.ds(first, hy, stride=2), :]) for t in range(2)
        ]
        pieces.append(jnp.concatenate(halves, axis=1))
    rhs = times(jnp.concatenate(pieces, axis=0), to_middle_z)
    for i in range(hx):
        mid[1, hx + i, T : T + hy, :] = rhs[i * hy : (i + 1) * hy]
    rhs_round = middle_start(1)

    def up(values):
        return jnp.concatenate([values[1:], values[:1]], axis=0)

    def down(values):
        return jnp.concatenate([values[-1:], values[:-1]], axis=0)

    def faces(k):
        return 0.5 * (k + up(k)), 0.5 * (k + shift(k, 1, 1)), 0.5 * (k + shift(k, 2, 1))

    def diagonal(w):
        return (w[0] + down(w[0])) + (w[1] + shift(w[1], 1, -1)) + (w[2] + shift(w[2], 2, -1))

    def neighbours(w, v):
        total = w[0] * up(v) + down(w[0] * v)
        total = total + (w[1] * shift(v, 1, 1) + shift(w[1] * v, 1, -1))
        return total + (w[2] * shift(v, 2, 1) + shift(w[2] * v, 2, -1))

    def sweep(w, inverse, v, f, omega):
        return (1.0 - omega) * v + omega * (f + neighbours(w, v)) * inverse

    def put_coeff(i, values):
        mk[i] = values

    middle_finish(0, coeff_round, put_coeff)
    mwx[0] = 0.5 * (mk[0] + mk[1])

    def middle_weights(i):
        set_weights(middle_w, lambda j: mk[j], i, middle_in & middle_plane_in(i))

    run(1, mx - 1, middle_weights)

    for copy in gather_coeff:
        copy.wait_recv()
    ck = cg[0, 0] + cg[0, 1]
    cshape = ck.shape
    row = iota(cshape, 1)
    plane = iota(cshape, 0)
    box_in = iota(cshape, 2) < 2 * qz
    nx, ny = 2 * qx, 2 * qy
    cw = faces(ck)
    half = 0.5 * ck
    cwx = jnp.where(plane < nx - 1, cw[0], 0.0)
    cwy = jnp.where(row < ny - 1, cw[1], 0.0)
    cw = (cwx, cwy, cw[2])
    cdiag = diagonal(cw)
    cdiag = cdiag + jnp.where(plane == 0, half, 0.0) + jnp.where(plane == nx - 1, half, 0.0)
    cdiag = cdiag + jnp.where(row == 0, half, 0.0) + jnp.where(row == ny - 1, half, 0.0)
    civ = jnp.where(box_in, 1.0 / cdiag, 0.0)

    finish_send(fine_round)
    finish_send(coeff_round)
    for copy in gather_coeff:
        copy.wait_send()

    def put_rhs(i, values):
        mf[i] = values
        if 1 <= i < mx - 1:
            va[i] = omega_first * values * miv[i]

    middle_finish(1, rhs_round, put_rhs)

    def middle_pre(i):
        vb[i] = plane_sweep(middle_w, mf[i], va, i, omega_second)

    def middle_leftover(i):
        va[i] = plane_left(middle_w, mf[i], vb, i)

    run(2, mx - 2, middle_pre)
    run(3, mx - 3, middle_leftover)

    pieces = []
    for i in range(qx):
        c = hx + 2 * i
        cs[i] = (va[c - 1] + va[c + 2]) * 0.5 + (va[c] + va[c + 1]) * 1.5
        pieces.append(restrict_rows(lambda first: cs[i, pl.ds(first, qy, stride=2), :]))
    rhs = times(jnp.concatenate(pieces, axis=0), to_coarse_z)
    for i in range(qx):
        cg[1, 0, px * qx + i, line, :] = rhs[i * qy : (i + 1) * qy]
    gather_rhs = gather_start(1)
    finish_send(rhs_round)
    for copy in gather_rhs:
        copy.wait_recv()

    cf = cg[1, 0] + cg[1, 1]
    c1 = omega_first * cf * civ
    c2 = sweep(cw, civ, c1, cf, omega_second)
    flat = c2.reshape(nx * ny, mz)
    correction = weigh(back_xy, times(flat, back_z))
    for i in range(hx):
        fixed = vb[hx + i, T : T + hy, :] + correction[i * hy : (i + 1) * hy]
        mid[2, hx + i, T : T + hy, :] = fixed
    last_round = middle_start(2)
    for copy in gather_rhs:
        copy.wait_send()
    finish_send(last_round)

    def put_last(i, values):
        vc[i] = values

    middle_finish(2, last_round, put_last)

    def middle_post_first(i):
        va[i] = plane_sweep(middle_w, mf[i], vc, i, omega_first)

    def middle_post_second(i):
        vb[i] = plane_sweep(middle_w, mf[i], va, i, omega_second)

    run(1, mx - 1, middle_post_first)
    run(2, mx - 2, middle_post_second)

    low = hx - 2
    spread = times(vb[low : 2 * hx + 2].reshape((hx + 4) * my, mz), to_fine_z)
    for i in range(2, ex - 2):
        c = (i - H + 64) // 2 - 32 + hx - low
        other = c - 1 if i % 2 == 0 else c + 1
        mixed = 0.75 * spread[c * my : (c + 1) * my] + 0.25 * spread[other * my : (other + 1) * my]
        near = 0.75 * mixed
        even = near + 0.25 * shift(mixed, 0, -1)
        odd = near + 0.25 * shift(mixed, 0, 1)
        for t in range(2):
            lanes = slice(t * cz_, (t + 1) * cz_)
            fs[t, i - 2, pl.ds(0, my, stride=2), :] = even[:, lanes]
            fs[t, i - 2, pl.ds(1, my, stride=2), :] = odd[:, lanes]
    for i in range(2, ex - 2):
        rows = slice(2 * T - T, 2 * T - T + ey)
        fresh = jnp.concatenate([fs[0, i - 2, rows, :], fs[1, i - 2, rows, :]], axis=1)
        ua[i] = jnp.where(fine_in & plane_in(i), ub[i] + fresh, 0.0)

    def post(i):
        ub[i] = plane_sweep(fine_w, ks[1, i], ua, i, omega_first)

    def last(i):
        result = plane_sweep(fine_w, ks[1, i], ub, i, omega_second)
        out_ref[i - H] = result[T : T + cy, 0:cz_]

    run(3, ex - 3, post)
    run(H, H + cx, last)


def solution(mesh):
    sizes = {axis: mesh.shape[axis] for axis in mesh.axis_names}
    spec = P("gx", "gy", "gz")

    def local(source, conductivity):
        cx, cy, cz = source.shape
        fine = (cx + 2 * H, cy + 2 * T, 2 * cz)
        mid = (cx // 2 * 3, cy // 2 + 2 * T, cz)
        vmem = pltpu.VMEM
        call = pl.pallas_call(
            functools.partial(kernel, sizes),
            out_shape=jax.ShapeDtypeStruct(source.shape, F32),
            in_specs=[pl.BlockSpec(memory_space=pltpu.HBM)] * 2,
            out_specs=pl.BlockSpec(memory_space=vmem),
            scratch_shapes=[
                vmem((2,) + fine, F32),
                vmem((cy, cz), F32),
                vmem((3, cy + 2 * T, cz), F32),
                vmem((3, cy + 2 * T, cz), F32),
                *[vmem(fine, F32)] * 8,
                vmem((2, cx // 2, cy + 2 * T, cz), F32),
                vmem((2, cx + 4, 2 * mid[1], cz), F32),
                vmem((cx // 4, mid[1], cz), F32),
                *[vmem(mid, F32)] * 10,
                vmem((3,) + mid, F32),
                vmem((3, cy // 2, cz), F32),
                vmem((3, 3) + mid[1:], F32),
                vmem((3, 3) + mid[1:], F32),
                vmem((2, 2, cx // 2, cy // 2, cz), F32),
                pltpu.SemaphoreType.DMA((copies,)),
                pltpu.SemaphoreType.DMA((copies,)),
                pltpu.SemaphoreType.DMA((2,)),
            ],
            compiler_params=pltpu.CompilerParams(
                collective_id=0, has_side_effects=True, vmem_limit_bytes=48 * 2**20
            ),
        )
        return call(*(pltpu.with_memory_space_constraint(v, pltpu.HBM) for v in (source, conductivity)))

    return jax.shard_map(
        local, mesh=mesh, in_specs=(spec, spec), out_specs=spec, check_vma=False
    )
```
